512 devices in a mesh: dp: 32 (over z, core), ctx: 16 (over x, y).
Axes of the slice: x: 4, y: 4, z: 16, core: 2. Of those that a mesh axis runs over, the one named last changes fastest.
Arguments:
- inputs: bfloat16 [65536, 512], P(('dp', 'ctx')), may hold values from -24 to 24
- attn_out: bfloat16 [65536, 512], P(('dp', 'ctx')), may hold values from -0.037353516 to 0.037353516
- out_grad: bfloat16 [65536, 512], P(('dp', 'ctx')), may hold values from -24 to 24
- w_uvqk: bfloat16 [512, 2048], replicated, may hold values from -0.25 to 0.25
- w_output: bfloat16 [512, 512], replicated, may hold values from -0.25 to 0.25
- norm_gain: float32 [512], replicated, may hold values from 0.1 to 1.9
- rab_table: float32 [8, 128], replicated, may hold values from -6 to 6
- bucket_map: int32 [1024], replicated, may hold values from 0 to 127, as said below
- lengths: int32 [32, 4], P('dp'), may hold values from 64 to 1024, as said below
- send_order: int32 [512, 128], P(('dp', 'ctx')), may hold values from 0 to 127, each once within a row
- recv_order: int32 [512, 128], P(('dp', 'ctx')), may hold values from 0 to 127, each once within a row
Outputs:
- grad_inputs: bfloat16 [65536, 512], P(('dp', 'ctx'))
- grad_uvqk: bfloat16 [512, 2048], P('ctx', 'dp')
- grad_output: bfloat16 [512, 512], P('ctx', 'dp')
The draws below stay inside these ranges and needn't reach their ends.
Inputs may be any that keep to these rules, and one draw needn't show every extreme that they name: `bucket_map`: nondecreasing in the distance, 0 at distance 0, every bucket taken. `lengths`: each row sums to 2048; its longest session has exactly 1024 events. `send_order`: each row is a permutation. `recv_order`: each row is a permutation.
All inputs are finite; a program needn't handle non-finite values.
Results may differ from the reference program's by a relative error of at most 0.019.
Values may be sent and summed in bfloat16 or wider, within the bound.
A program may use at most 128 MiB of HBM per device.

```python
import jax
import jax.numpy as jnp
from jax import lax

D = 512
H = 8
DH = 64
NB = 128
SESS = 4
ROWS = 128
TOKENS = 65536
GROUP = 2048
MOST = 1024
SPAN = 1024
SHARE = 4
N_DP = 32
N_CTX = 16
DEVICES = 512


def draw_bucket_map(key, part):
    key = jax.random.fold_in(key, 11)
    breaks = jax.random.permutation(key, MOST - 1)[:NB - 1].astype(jnp.int32) + 1
    distance = jnp.arange(MOST, dtype=jnp.int32)
    return jnp.sum((distance[:, None] >= breaks[None, :]).astype(jnp.int32), axis=1).astype(jnp.int32)


def one_row(row_key):
    floor_len = min(64, (GROUP - MOST) // (SESS - 1))
    extra = GROUP - MOST - (SESS - 1) * floor_len
    cut_key, order_key = jax.random.split(row_key)
    cuts = jnp.sort(jax.random.randint(cut_key, (SESS - 3,), 0, extra + 1)).astype(jnp.int32)
    edges = jnp.concatenate([jnp.zeros((1,), jnp.int32), cuts, jnp.full((1,), extra, jnp.int32)])
    gaps = (edges[1:] - edges[:-1]).astype(jnp.int32)
    row = jnp.concatenate([jnp.full((1,), MOST, jnp.int32), jnp.full((1,), floor_len, jnp.int32), floor_len + gaps]).astype(jnp.int32)
    return jax.random.permutation(order_key, row).astype(jnp.int32)


def draw_lengths(key, part):
    key = jax.random.fold_in(key, 23)
    row_keys = jax.random.split(key, N_DP)
    return jax.vmap(one_row)(row_keys).astype(jnp.int32)


def strengthened(drawn, stream_key, source, target, parts, factor):
    def block_of(axis_at):
        return (jnp.arange(drawn.shape[axis_at]) // (drawn.shape[axis_at] // parts)).reshape((-1,) + (1,) * (drawn.ndim - 1 - axis_at))

    first = jax.random.permutation(stream_key, parts)[block_of(target)]
    far = (block_of(target) + parts // 2) % parts
    return jnp.where((block_of(source) == first) | (block_of(source) == far), factor * drawn, drawn)


def steps_of(key, dims, cuts, least, top_value):
    def one(dim, blocks):
        heights = jax.random.uniform(jax.random.fold_in(jax.random.fold_in(key, 6), dim), (blocks,), jnp.float32, least / len(cuts), top_value / len(cuts))
        return jnp.repeat(jnp.exp(heights), dims[dim] // blocks).reshape((-1,) + (1,) * (len(dims) - dim - 1))

    level = one(*cuts[0])
    for cut in cuts[1:]:
        level = level * one(*cut)
    return level


def scatter_about(rng, shape, spread, bound, cuts=(), held_as=jnp.bfloat16):
    drawn = jax.random.normal(rng, shape, jnp.float32) * spread
    if len(cuts) > 0:
        drawn = steps_of(rng, shape, cuts, -0.22, 0.18) * drawn
    return jnp.clip(drawn, min=-bound, max=bound).astype(held_as)


def bell_draw_with(own_key, dims, spread, most, cuts, heavy, kind=jnp.bfloat16):
    drawn = spread * jax.random.normal(own_key, dims, jnp.float32)
    if cuts:
        drawn = drawn * steps_of(own_key, dims, cuts, -0.22, 0.18)
    return jnp.clip(strengthened(drawn, jax.random.fold_in(own_key, 3), *heavy), -most, most).astype(kind)


def setup_inputs(seed: int = 0) -> dict:
    key_list = jax.random.split(jax.random.key(seed), 12)
    inputs = bell_draw_with(key_list[0], (TOKENS, D), 1.0, 24.0, ((0, 512),), (0, 1, 512, 6.0))
    attn_out = scatter_about(key_list[1], (TOKENS, D), 0.00625, 0.037353516, ((0, 512),))
    out_grad = bell_draw_with(key_list[2], (TOKENS, D), 1.0, 24.0, ((0, 512),), (0, 1, 512, 6.0))
    w_uvqk = scatter_about(key_list[3], (D, 4 * D), D ** -0.5, 0.25)
    w_output = scatter_about(key_list[4], (D, D), D ** -0.5, 0.25)
    norm_gain = jnp.clip(1.0 + 0.18 * jax.random.normal(key_list[5], (D,), jnp.float32), 0.1, 1.9)
    rab_table = scatter_about(key_list[6], (H, NB), 1.0, 6.0, (), jnp.float32)
    bucket_map = draw_bucket_map(jax.random.fold_in(key_list[11], 71), 0)
    lengths = draw_lengths(jax.random.fold_in(key_list[11], 71), 0)
    send_order = jax.vmap(lambda own: jax.random.permutation(own, ROWS))(jax.random.split(key_list[9], DEVICES)).reshape((DEVICES, ROWS)).astype(jnp.int32)
    recv_order = jax.vmap(lambda own: jax.random.permutation(own, ROWS))(jax.random.split(key_list[10], DEVICES)).reshape((DEVICES, ROWS)).astype(jnp.int32)
    return {"inputs": inputs, "attn_out": attn_out, "out_grad": out_grad, "w_uvqk": w_uvqk, "w_output": w_output, "norm_gain": norm_gain, "rab_table": rab_table, "bucket_map": bucket_map, "lengths": lengths, "send_order": send_order, "recv_order": recv_order}


norm_eps = 1e-05

def rounded(array):
    return lax.optimization_barrier(array.astype(jnp.bfloat16))

def silu_slope(array):
    squash = jax.nn.sigmoid(array)
    return squash * (1.0 + array * (1.0 - squash))

def session_of(positions, bounds):
    return lax.optimization_barrier(jnp.sum((positions[:, None] >= bounds[None, :-1]).astype(jnp.int32), axis=1)).astype(jnp.int32)

def group_attention(group_pack, dist_bias):
    queries, key_rows, values, grads, lengths_row = group_pack
    bounds = jnp.cumsum(lengths_row).astype(jnp.int32)
    positions = jnp.arange(GROUP, dtype=jnp.int32)
    sessions = session_of(positions, bounds)
    query_heads = queries.astype(jnp.float32).reshape(GROUP, H, DH)
    key_heads = key_rows.astype(jnp.float32).reshape(GROUP, H, DH)
    value_heads = values.astype(jnp.float32).reshape(GROUP, H, DH)
    grad_heads = grads.astype(jnp.float32).reshape(GROUP, H, DH)
    block_rows = min(512, GROUP)
    score_scale = DH ** (-0.5)

    def step_block(totals, block_index):
        acc_keys, acc_values = totals
        first_row = block_index * block_rows
        query_block = lax.dynamic_slice_in_dim(query_heads, first_row, block_rows, 0)
        grad_block = lax.dynamic_slice_in_dim(grad_heads, first_row, block_rows, 0)
        block_pos = first_row + jnp.arange(block_rows, dtype=jnp.int32)
        block_sess = lax.dynamic_slice_in_dim(sessions, first_row, block_rows, 0)
        distance = block_pos[:, None] - positions[None, :]
        allowed = (distance >= 0) & (block_sess[:, None] == sessions[None, :])
        bias_tile = dist_bias[:, jnp.clip(distance, 0, MOST - 1)]
        scores = jnp.einsum('ihd,jhd->hij', query_block, key_heads) * score_scale + bias_tile
        squash = jax.nn.sigmoid(scores)
        weights = rounded(jnp.where(allowed[None], scores * squash / SPAN, 0.0)).astype(jnp.float32)
        effect = jnp.einsum('ihd,jhd->hij', grad_block, value_heads) / SPAN
        slopes = rounded(jnp.where(allowed[None], effect * squash * (1.0 + scores * (1.0 - squash)), 0.0)).astype(jnp.float32)
        grad_query = jnp.einsum('hij,jhd->ihd', slopes, key_heads)
        acc_keys = acc_keys + jnp.einsum('hij,ihd->jhd', slopes, query_block)
        acc_values = acc_values + jnp.einsum('hij,ihd->jhd', weights, grad_block)
        return ((acc_keys, acc_values), grad_query)
    zero_heads = jnp.zeros((GROUP, H, DH), jnp.float32)
    totals, grad_blocks = lax.scan(step_block, (zero_heads, zero_heads), jnp.arange(GROUP // block_rows, dtype=jnp.int32))
    grad_query = grad_blocks.reshape(GROUP, D) * score_scale
    grad_key = totals[0].reshape(GROUP, D) * score_scale
    return (grad_query, grad_key, totals[1].reshape(GROUP, D))

def reference(inputs, attn_out, out_grad, w_uvqk, w_output, norm_gain, rab_table, bucket_map, lengths, send_order, recv_order):
    pre_act = jnp.dot(inputs, w_uvqk, preferred_element_type=jnp.float32)
    activated = rounded(jax.nn.silu(pre_act))
    gating = activated[:, :D]
    values = activated[:, D:2 * D]
    queries = activated[:, 2 * D:3 * D]
    key_rows = activated[:, 3 * D:]
    owner_rows = jnp.arange(TOKENS, dtype=jnp.int32)
    owner_dev = owner_rows // ROWS
    owner_grp = owner_dev // N_CTX
    owner_ctx = owner_dev % N_CTX
    slot_ids = recv_order.reshape(-1)[owner_rows]
    source_dev = slot_ids // SHARE * N_CTX + owner_ctx
    source_rows = source_dev * ROWS + send_order.reshape(-1)[source_dev * ROWS + owner_grp * SHARE + slot_ids % SHARE]
    owned_grad = out_grad[source_rows]
    grad_z = jnp.dot(owned_grad, w_output.T, preferred_element_type=jnp.float32)
    attn_f = attn_out.astype(jnp.float32)
    centred = attn_f - lax.optimization_barrier(jnp.mean(attn_f, axis=1, keepdims=True))
    inv_std = lax.rsqrt(lax.optimization_barrier(jnp.mean(centred * centred, axis=1, keepdims=True)) + norm_eps)
    normal_hat = centred * inv_std
    normed = normal_hat * norm_gain
    gating_f = gating.astype(jnp.float32)
    mixed_z = rounded(normed * gating_f)
    grad_gate = grad_z * normed
    grad_hat = grad_z * gating_f * norm_gain
    grad_attn = rounded((grad_hat - lax.optimization_barrier(jnp.mean(grad_hat, axis=1, keepdims=True)) - normal_hat * lax.optimization_barrier(jnp.mean(grad_hat * normal_hat, axis=1, keepdims=True))) * inv_std)
    dist_bias = rab_table[:, bucket_map]
    packed = (queries.reshape(N_DP, GROUP, D), key_rows.reshape(N_DP, GROUP, D), values.reshape(N_DP, GROUP, D), grad_attn.reshape(N_DP, GROUP, D), lengths)
    grad_query, grad_key, grad_value = lax.map(lambda group_pack: group_attention(group_pack, dist_bias), packed)
    grad_all = jnp.concatenate([grad_gate, grad_value.reshape(TOKENS, D), grad_query.reshape(TOKENS, D), grad_key.reshape(TOKENS, D)], axis=1)
    grad_pre = rounded(grad_all * silu_slope(pre_act))
    branch = rounded(jnp.dot(grad_pre, w_uvqk.T, preferred_element_type=jnp.float32))
    placed = jnp.zeros((TOKENS, D), jnp.float32).at[source_rows].set(branch.astype(jnp.float32))
    grad_inputs = (out_grad.astype(jnp.float32) + placed).astype(jnp.bfloat16)
    device_items = (inputs.reshape(DEVICES, ROWS, D), grad_pre.reshape(DEVICES, ROWS, 4 * D), mixed_z.reshape(DEVICES, ROWS, D), owned_grad.reshape(DEVICES, ROWS, D))

    def add_term(totals, members):
        input_block, grad_block, mixed_block, owned_block = members
        upper_part = jnp.dot(input_block.T, grad_block, preferred_element_type=jnp.float32)
        lower_part = jnp.dot(mixed_block.T, owned_block, preferred_element_type=jnp.float32)
        term = rounded(jnp.concatenate([upper_part, lower_part], axis=1)).astype(jnp.float32)
        return (totals + term, None)
    summed, unused = lax.scan(add_term, jnp.zeros((D, 5 * D), jnp.float32), device_items)
    grad_scale = TOKENS ** (-0.5)
    return (grad_inputs, (summed[:, :4 * D] * grad_scale).astype(jnp.bfloat16), (summed[:, 4 * D:] * grad_scale).astype(jnp.bfloat16))
```

```python
import jax
import jax.numpy as jnp
from jax import lax
from jax.experimental import pallas as pl
from jax.experimental.pallas import tpu as pltpu
from jax.sharding import PartitionSpec as P

MESH = pl.DeviceIdType.MESH
F32 = jnp.float32
BF16 = jnp.bfloat16

D = 512
H = 8
ROWS = 128
N_DP = 32
N_CTX = 16
N_Z = 16
TILES = 16
REACH = 8
HALF = 8
SLOTS = 512
TERM_COLS = 1280
EPS = 1e-05
LIMIT = 40 * 1024 * 1024


def mm(left, right, dims=((1,), (0,))):
    return lax.dot_general(left, right, (dims, ((), ())), preferred_element_type=F32)


def iota(shape, dim):
    return lax.broadcasted_iota(jnp.int32, shape, dim)


def slot_of(place):
    return (place >> 4) * 4 + (place & 3)


def piece_of(place):
    return (place >> 2) & 3


def sigmoid(array):
    return 1.0 / (1.0 + jnp.exp(-array))


def half_of(ctx):
    return lax.rem((ctx + 1) // 2, 2)


def member(index, half):
    return 2 * index + lax.rem(half + index, 2)


def by_piece(wide):
    piece = piece_of(iota((SLOTS, 128), 0))
    out = wide[:, :128]
    for part in range(1, 4):
        out = jnp.where(piece == part, wide[:, part * 128 : part * 128 + 128], out)
    return out


def pick_pieces(hot, flat):
    piece = piece_of(iota(hot.shape, 1))
    parts = [mm(jnp.where(piece == part, hot, 0.0).astype(BF16), flat) for part in range(4)]
    return jnp.concatenate(parts, axis=1)


def swap(array):
    return pltpu.roll(array, 64, 1)


def announce(me_dp, me_ctx):
    barrier = pltpu.get_barrier_semaphore()

    def tell_dp(step, carry):
        peer = lax.rem(me_dp + step, N_DP)
        pl.semaphore_signal(barrier, inc=1, device_id=(peer, me_ctx), device_id_type=MESH)
        return carry

    def tell_ctx(step, carry):
        peer = lax.rem(me_ctx + step, N_CTX)
        pl.semaphore_signal(barrier, inc=1, device_id=(me_dp, peer), device_id_type=MESH)
        return carry

    lax.fori_loop(1, N_DP, tell_dp, 0)
    lax.fori_loop(1, N_CTX, tell_ctx, 0)


def everyone_in():
    pl.semaphore_wait(pltpu.get_barrier_semaphore(), N_DP - 1 + N_CTX - 1)


def spread(count, copy_to):
    def one(step, carry):
        copy_to(step).start()
        return carry

    lax.fori_loop(1, count, one, 0)


def front_kernel(
    x_ref,
    attn_ref,
    og_ref,
    w_ref,
    wo_ref,
    gain_ref,
    rab_ref,
    bm_ref,
    so_ref,
    ro_ref,
    kv_out,
    qg_out,
    bias_out,
    gate_out,
    mixed_out,
    owned_out,
    sorted_rows,
    arrived,
    kv_send,
    qg_send,
    send_sem,
    recv_sem,
):
    me_dp = lax.axis_index("dp")
    me_ctx = lax.axis_index("ctx")
    half = half_of(me_ctx)
    announce(me_dp, me_ctx)
    low = iota((ROWS, 128), 1) < 64

    order = so_ref[...].astype(F32)
    lane = iota((SLOTS, 128), 1)
    place = iota((SLOTS, 128), 0)
    wanted = jnp.sum(jnp.where(lane == slot_of(place), order, 0.0), axis=1, keepdims=True)
    hot = jnp.where(lane.astype(F32) == wanted, 1.0, 0.0).astype(BF16)
    sorted_rows[...] = by_piece(mm(hot, og_ref[...])).astype(BF16).reshape(N_DP, 16, 128)
    arrived[me_dp] = sorted_rows[me_dp]
    everyone_in()

    def row_copy(step):
        peer = lax.rem(me_dp + step, N_DP)
        return pltpu.make_async_remote_copy(
            src_ref=sorted_rows.at[peer],
            dst_ref=arrived.at[me_dp],
            send_sem=send_sem.at[0],
            recv_sem=recv_sem.at[0],
            device_id=(peer, me_ctx),
            device_id_type=MESH,
        )

    spread(N_DP, row_copy)

    x = x_ref[...]
    pre_v = mm(x, w_ref[:, D : 2 * D])
    pre_k = mm(x, w_ref[:, 3 * D :])
    value = pre_v * sigmoid(pre_v)
    key = pre_k * sigmoid(pre_k)
    for pair in range(H // 2):
        k_two = key[:, pair * 128 : pair * 128 + 128]
        v_two = value[:, pair * 128 : pair * 128 + 128]
        kv_send[2 * pair] = jnp.where(low, k_two, swap(v_two)).astype(BF16)
        kv_send[2 * pair + 1] = jnp.where(low, swap(k_two), v_two).astype(BF16)
    kv_out[me_ctx] = kv_send[me_ctx // 2]

    def kv_copy(step):
        peer = lax.rem(me_ctx + step, N_CTX)
        return pltpu.make_async_remote_copy(
            src_ref=kv_send.at[peer // 2],
            dst_ref=kv_out.at[me_ctx],
            send_sem=send_sem.at[1],
            recv_sem=recv_sem.at[1],
            device_id=(me_dp, peer),
            device_id_type=MESH,
        )

    spread(N_CTX, kv_copy)

    pre_u = mm(x, w_ref[:, :D])
    pre_q = mm(x, w_ref[:, 2 * D : 3 * D])
    sig_u = sigmoid(pre_u)
    gating = (pre_u * sig_u).astype(BF16).astype(F32)
    slope_u = sig_u * (1.0 + pre_u * (1.0 - sig_u))
    query = (pre_q * sigmoid(pre_q)).astype(BF16).astype(F32) * 0.0625
    gain = gain_ref[...]
    attn = attn_ref[...].astype(F32)
    centred = attn - jnp.mean(attn, axis=1, keepdims=True)
    inv_std = lax.rsqrt(jnp.mean(centred * centred, axis=1, keepdims=True) + EPS)
    normal_hat = centred * inv_std
    normed = normal_hat * gain
    mixed_out[...] = (normed * gating).astype(BF16)
    gate_scale = normed * slope_u
    hat_scale = gating * gain

    buckets = iota((128, 128), 0)
    tables = []
    for block in range(REACH):
        chosen = jnp.where(buckets == bm_ref[block : block + 1, :], 1.0, 0.0)
        tables.append(
            lax.dot_general(
                rab_ref[...],
                chosen,
                (((1,), (0,)), ((), ())),
                precision=lax.Precision.HIGHEST,
                preferred_element_type=F32,
            )
        )
    own_head = iota((H, 128), 0) == me_ctx // 2
    lines = [
        jnp.sum(jnp.where(own_head, table, 0.0), axis=0, keepdims=True) * 0.5 for table in tables
    ]
    blank = jnp.zeros((1, 128), F32)
    for far in range(REACH + 1):
        current = lines[far] if far < REACH else blank
        before = lines[far - 1] if far > 0 else blank
        both = jnp.broadcast_to(jnp.concatenate([current, before], axis=1), (128, 256))
        tile = pltpu.roll(both, 0, 1, stride=1, stride_axis=0)[:, :128]
        bias_out[(REACH - far) * 128 : (REACH - far) * 128 + 128, :] = tile

    taken = ro_ref[...].astype(F32)
    square = iota((128, 128), 0) == iota((128, 128), 1)
    slot_col = jnp.sum(jnp.where(square, taken, 0.0), axis=1, keepdims=True)
    place = iota((ROWS, SLOTS), 1)
    hot = jnp.where(slot_of(place).astype(F32) == slot_col, 1.0, 0.0)

    row_wait = pltpu.make_async_remote_copy(
        src_ref=sorted_rows.at[pl.ds(0, N_DP - 1)],
        dst_ref=arrived.at[pl.ds(0, N_DP - 1)],
        send_sem=send_sem.at[0],
        recv_sem=recv_sem.at[0],
        device_id=(lax.rem(me_dp + 1, N_DP), me_ctx),
        device_id_type=MESH,
    )
    row_wait.wait_recv()
    owned = pick_pieces(hot, arrived[...].reshape(SLOTS, 128)).astype(BF16)
    owned_out[...] = owned
    grad_z = mm(owned, wo_ref[...], ((1,), (1,)))
    grad_hat = grad_z * hat_scale
    grad_attn = (
        grad_hat
        - jnp.mean(grad_hat, axis=1, keepdims=True)
        - normal_hat * jnp.mean(grad_hat * normal_hat, axis=1, keepdims=True)
    ) * inv_std
    for pair in range(H // 2):
        q_two = query[:, pair * 128 : pair * 128 + 128]
        g_two = grad_attn[:, pair * 128 : pair * 128 + 128]
        qg_send[2 * pair] = jnp.where(low, q_two, swap(g_two)).astype(BF16)
        qg_send[2 * pair + 1] = jnp.where(low, swap(q_two), g_two).astype(BF16)
    own = me_ctx // 2
    qg_out[own] = qg_send[own]

    def qg_copy(step):
        head = lax.rem(own + step, HALF)
        return pltpu.make_async_remote_copy(
            src_ref=qg_send.at[head],
            dst_ref=qg_out.at[own],
            send_sem=send_sem.at[2],
            recv_sem=recv_sem.at[2],
            device_id=(me_dp, member(head, half)),
            device_id_type=MESH,
        )

    spread(HALF, qg_copy)
    gate_out[...] = (grad_z * gate_scale).astype(BF16)

    kv_wait = pltpu.make_async_remote_copy(
        src_ref=kv_out.at[pl.ds(0, N_CTX - 1)],
        dst_ref=kv_out.at[pl.ds(0, N_CTX - 1)],
        send_sem=send_sem.at[1],
        recv_sem=recv_sem.at[1],
        device_id=(me_dp, lax.rem(me_ctx + 1, N_CTX)),
        device_id_type=MESH,
    )
    qg_wait = pltpu.make_async_remote_copy(
        src_ref=qg_send.at[pl.ds(0, HALF - 1)],
        dst_ref=qg_out.at[pl.ds(0, HALF - 1)],
        send_sem=send_sem.at[2],
        recv_sem=recv_sem.at[2],
        device_id=(me_dp, lax.rem(me_ctx + 1, N_CTX)),
        device_id_type=MESH,
    )
    kv_wait.wait_recv()
    qg_wait.wait_recv()
    row_wait.wait_send()
    kv_wait.wait_send()
    qg_wait.wait_send()


def attend_kernel(len_ref, kv_ref, qg_ref, bias_ref, dkv_out, dqt_out, padded, turned, totals, turned_total):
    half = half_of(lax.axis_index("ctx"))
    pad_rows = REACH * 128
    padded[:pad_rows, :] = jnp.zeros((pad_rows, 128), BF16)
    turned[:, :pad_rows] = jnp.zeros((64, pad_rows), BF16)
    totals[...] = jnp.zeros(totals.shape, F32)
    for tile in range(TILES):
        block = kv_ref[tile]
        padded[pad_rows + tile * 128 : pad_rows + tile * 128 + 128, :] = block
        flipped = block.astype(F32).T
        turned[:, pad_rows + tile * 128 : pad_rows + tile * 128 + 128] = flipped[:64].astype(BF16)
    edge_one = len_ref[0, 0]
    edge_two = edge_one + len_ref[0, 1]
    edge_three = edge_two + len_ref[0, 2]

    def begin(place, choose):
        first = choose(place >= edge_one, edge_one, 0)
        first = choose(place >= edge_two, edge_two, first)
        return choose(place >= edge_three, edge_three, first)

    low = iota((128, 128), 1) < 64

    def one_tile(index, carry):
        tile = member(index, half)
        qg = qg_ref[index].astype(F32)
        pair = jnp.concatenate([jnp.where(low, qg, 0.0), jnp.where(low, 0.0, qg)], axis=0).astype(
            BF16
        )
        place = tile * 128 + iota((1, 128), 1)
        first = begin(place, jnp.where)
        least = begin(tile * 128, jnp.where)

        def group(step):
            row = pl.multiple_of((tile - 3 * step - 2 + REACH) * 128, 128)
            keys = padded[pl.ds(row, 384), :]
            both = mm(keys, pair, ((1,), (1,)))
            scores = both[:, :128] + bias_ref[(6 - 3 * step) * 128 : (9 - 3 * step) * 128, :]
            bent = jnp.tanh(scores)
            rise = 1.0 + bent
            weights = scores * rise
            slopes = both[:, 128:] * (rise + weights * (1.0 - bent))
            key_place = row - pad_rows + iota((384, 128), 0)
            allowed = key_place >= first
            if step == 0:
                allowed = allowed & (key_place <= place)
            weights = jnp.where(allowed, weights, 0.0).astype(BF16)
            slopes = jnp.where(allowed, slopes, 0.0).astype(BF16)
            totals[pl.ds(row, 384), :] += mm(jnp.concatenate([slopes, weights], axis=1), pair)
            return mm(turned[:, pl.ds(row, 384)], slopes)

        turned_total[...] = group(0)
        for step in (1, 2):

            @pl.when((tile - 3 * step) * 128 + 127 >= least)
            def _():
                turned_total[...] += group(step)

        dqt_out[index] = (turned_total[...] * (1.0 / 16384.0)).astype(BF16)
        return carry

    lax.fori_loop(0, HALF, one_tile, 0)
    for tile in range(TILES):
        rows = totals[pad_rows + tile * 128 : pad_rows + tile * 128 + 128, :]
        dkv_out[tile] = (rows * (1.0 / 1024.0)).astype(BF16)


def back_kernel(
    x_ref,
    og_ref,
    w_ref,
    so_ref,
    ro_ref,
    dkv_ref,
    dqt_ref,
    gate_ref,
    mixed_ref,
    owned_ref,
    rows_out,
    uvqk_out,
    output_out,
    kv_got,
    q_got,
    back_rows,
    returned,
    other_x,
    other_mixed,
    other_owned,
    other_pre,
    owned_send,
    pre_send,
    terms,
    terms_got,
    last_send,
    last_got,
    send_sem,
    recv_sem,
):
    me_dp = lax.axis_index("dp")
    me_ctx = lax.axis_index("ctx")
    core = lax.rem(me_dp, 2)
    me_z = me_dp // 2
    half = half_of(me_ctx)
    own = me_ctx // 2
    partner = me_dp + 1 - 2 * core
    announce(me_dp, me_ctx)
    low = iota((ROWS, 128), 1) < 64

    def to_partner(source, target, number):
        return pltpu.make_async_remote_copy(
            src_ref=source,
            dst_ref=target,
            send_sem=send_sem.at[number],
            recv_sem=recv_sem.at[number],
            device_id=(partner, me_ctx),
            device_id_type=MESH,
        )

    owned = owned_ref[...]
    column = iota((D, 256), 1)
    source_row = iota((D, 256), 0)
    spread_col = (column >> 4) * 32 + (column & 15)
    owned_own = mm(owned, jnp.where(source_row == spread_col + 16 * core, 1.0, 0.0).astype(BF16))
    owned_else = mm(
        owned, jnp.where(source_row == spread_col + 16 * (1 - core), 1.0, 0.0).astype(BF16)
    )
    owned_send[...] = owned_else.astype(BF16)
    kv_got[me_ctx] = dkv_ref[me_ctx]
    q_got[own] = dqt_ref[own]
    everyone_in()

    def kv_copy(step):
        peer = lax.rem(me_ctx + step, N_CTX)
        return pltpu.make_async_remote_copy(
            src_ref=dkv_ref.at[peer],
            dst_ref=kv_got.at[me_ctx],
            send_sem=send_sem.at[4],
            recv_sem=recv_sem.at[4],
            device_id=(me_dp, peer),
            device_id_type=MESH,
        )

    def q_copy(step):
        index = lax.rem(own + step, HALF)
        return pltpu.make_async_remote_copy(
            src_ref=dqt_ref.at[index],
            dst_ref=q_got.at[own],
            send_sem=send_sem.at[5],
            recv_sem=recv_sem.at[5],
            device_id=(me_dp, member(index, half)),
            device_id_type=MESH,
        )

    spread(N_CTX, kv_copy)
    spread(HALF, q_copy)
    x_copy = to_partner(x_ref, other_x, 0)
    mixed_copy = to_partner(mixed_ref, other_mixed, 1)
    owned_copy = to_partner(owned_send, other_owned, 2)
    x_copy.start()
    mixed_copy.start()
    owned_copy.start()

    x = x_ref[...]
    pre = mm(x, w_ref[:, D:])
    squash = sigmoid(pre)
    slope = squash * (1.0 + pre * (1.0 - squash))

    slot = slot_of(iota((SLOTS, ROWS), 0))
    back_hot = jnp.where(slot == ro_ref[...], 1.0, 0.0).astype(BF16)
    sent = jnp.where(iota((ROWS, 128), 0) == so_ref[...], 1.0, 0.0).astype(BF16)
    place = iota((ROWS, SLOTS), 1)
    spot = jnp.where(iota((ROWS, SLOTS), 0) == slot_of(place), 1.0, 0.0).astype(BF16)
    final_hot = mm(sent, spot)

    kv_wait = pltpu.make_async_remote_copy(
        src_ref=dkv_ref.at[pl.ds(0, N_CTX - 1)],
        dst_ref=kv_got.at[pl.ds(0, N_CTX - 1)],
        send_sem=send_sem.at[4],
        recv_sem=recv_sem.at[4],
        device_id=(me_dp, lax.rem(me_ctx + 1, N_CTX)),
        device_id_type=MESH,
    )
    q_wait = pltpu.make_async_remote_copy(
        src_ref=dqt_ref.at[pl.ds(0, HALF - 1)],
        dst_ref=q_got.at[pl.ds(0, HALF - 1)],
        send_sem=send_sem.at[5],
        recv_sem=recv_sem.at[5],
        device_id=(me_dp, lax.rem(me_ctx + 1, N_CTX)),
        device_id_type=MESH,
    )
    kv_wait.wait_recv()
    q_wait.wait_recv()
    grad_k = []
    grad_v = []
    for pair in range(H // 2):
        even = kv_got[4 * pair].astype(F32) + kv_got[4 * pair + 1].astype(F32)
        odd = kv_got[4 * pair + 2].astype(F32) + kv_got[4 * pair + 3].astype(F32)
        grad_k.append(jnp.where(low, even, swap(odd)))
        grad_v.append(jnp.where(low, swap(even), odd))
    grad_q = q_got[...].reshape(D, 128).astype(F32).T
    after = jnp.concatenate(grad_v + [grad_q] + grad_k, axis=1) * slope
    gate = gate_ref[...]
    grad_pre = jnp.concatenate([gate, after.astype(BF16)], axis=1)

    branch = mm(grad_pre, w_ref[...], ((1,), (1,))).astype(BF16)
    back_rows[...] = by_piece(mm(back_hot, branch)).astype(BF16).reshape(N_DP, 16, 128)
    returned[me_dp] = back_rows[me_dp]

    def row_copy(step):
        peer = lax.rem(me_dp + step, N_DP)
        return pltpu.make_async_remote_copy(
            src_ref=back_rows.at[peer],
            dst_ref=returned.at[me_dp],
            send_sem=send_sem.at[6],
            recv_sem=recv_sem.at[6],
            device_id=(peer, me_ctx),
            device_id_type=MESH,
        )

    spread(N_DP, row_copy)

    full = jnp.concatenate([gate.astype(F32), after], axis=1)
    zero_core = jnp.broadcast_to(core, (ROWS, 128)) == 0
    mine = []
    for block in range(8):
        first = full[:, 256 * block : 256 * block + 128]
        second = full[:, 256 * block + 128 : 256 * block + 256]
        even = jnp.where(low, first, swap(second))
        odd = jnp.where(low, swap(first), second)
        mine.append(jnp.where(zero_core, even, odd).astype(BF16))
        pre_send[:, 128 * block : 128 * block + 128] = jnp.where(zero_core, odd, even).astype(BF16)
    pre_copy = to_partner(pre_send, other_pre, 3)
    pre_copy.start()
    x_copy.wait_recv()
    mixed_copy.wait_recv()
    owned_copy.wait_recv()
    x_both = jnp.concatenate([x, other_x[...]], axis=0)
    mixed_both = jnp.concatenate([mixed_ref[...], other_mixed[...]], axis=0)
    owned_both = jnp.concatenate([owned_own.astype(BF16), other_owned[...]], axis=0)
    lower = mm(mixed_both, owned_both, ((0,), (0,)))
    terms[:, :, 1024:] = lower.astype(BF16).reshape(N_CTX, 32, 256)
    pre_copy.wait_recv()
    pre_both = jnp.concatenate([jnp.concatenate(mine, axis=1), other_pre[...]], axis=0)
    upper = mm(x_both, pre_both, ((0,), (0,)))
    terms[:, :, :1024] = upper.astype(BF16).reshape(N_CTX, 32, 1024)
    terms_got[me_ctx] = terms[me_ctx]

    def term_copy(step):
        peer = lax.rem(me_ctx + step, N_CTX)
        return pltpu.make_async_remote_copy(
            src_ref=terms.at[peer],
            dst_ref=terms_got.at[me_ctx],
            send_sem=send_sem.at[7],
            recv_sem=recv_sem.at[7],
            device_id=(me_dp, peer),
            device_id_type=MESH,
        )

    spread(N_CTX, term_copy)

    row_wait = pltpu.make_async_remote_copy(
        src_ref=back_rows.at[pl.ds(0, N_DP - 1)],
        dst_ref=returned.at[pl.ds(0, N_DP - 1)],
        send_sem=send_sem.at[6],
        recv_sem=recv_sem.at[6],
        device_id=(lax.rem(me_dp + 1, N_DP), me_ctx),
        device_id_type=MESH,
    )
    row_wait.wait_recv()
    arrival = pick_pieces(final_hot, returned[...].reshape(SLOTS, 128))
    rows_out[...] = (og_ref[...].astype(F32) + arrival).astype(BF16)

    term_wait = pltpu.make_async_remote_copy(
        src_ref=terms.at[pl.ds(0, N_CTX - 1)],
        dst_ref=terms_got.at[pl.ds(0, N_CTX - 1)],
        send_sem=send_sem.at[7],
        recv_sem=recv_sem.at[7],
        device_id=(me_dp, lax.rem(me_ctx + 1, N_CTX)),
        device_id_type=MESH,
    )
    term_wait.wait_recv()
    summed = terms_got[0].astype(F32)
    for source in range(1, N_CTX):
        summed = summed + terms_got[source].astype(F32)

    low = iota((32, 128), 1) < 64
    for index in range(N_Z):
        block = summed[:, (index // 2) * 128 : (index // 2) * 128 + 128]
        if index % 2 == 1:
            block = swap(block)
        start = 1024 + (index // 8) * 128
        extra = summed[:, start : start + 128]
        shift = (64 - 16 * (index % 8)) % 128
        if shift:
            extra = pltpu.roll(extra, shift, 1)
        last_send[index] = jnp.where(low, block, extra).astype(BF16)
    last_got[me_z] = last_send[me_z]

    def last_copy(step):
        peer = lax.rem(me_z + step, N_Z)
        return pltpu.make_async_remote_copy(
            src_ref=last_send.at[peer],
            dst_ref=last_got.at[me_z],
            send_sem=send_sem.at[8],
            recv_sem=recv_sem.at[8],
            device_id=(2 * peer + core, me_ctx),
            device_id_type=MESH,
        )

    spread(N_Z, last_copy)
    last_wait = pltpu.make_async_remote_copy(
        src_ref=last_send.at[pl.ds(0, N_Z - 1)],
        dst_ref=last_got.at[pl.ds(0, N_Z - 1)],
        send_sem=send_sem.at[8],
        recv_sem=recv_sem.at[8],
        device_id=(2 * lax.rem(me_z + 1, N_Z) + core, me_ctx),
        device_id_type=MESH,
    )
    last_wait.wait_recv()
    total = last_got[0].astype(F32)
    for source in range(1, N_Z):
        total = total + last_got[source].astype(F32)
    total = (total * (1.0 / 256.0)).astype(BF16)
    uvqk_out[...] = total[:, :64]
    output_out[...] = total[:, 64:80]
    kv_wait.wait_send()
    q_wait.wait_send()
    x_copy.wait_send()
    mixed_copy.wait_send()
    owned_copy.wait_send()
    pre_copy.wait_send()
    row_wait.wait_send()
    term_wait.wait_send()
    last_wait.wait_send()


def in_vmem(count):
    return [pl.BlockSpec(memory_space=pltpu.VMEM)] * count


def bf16(*shape):
    return jax.ShapeDtypeStruct(shape, BF16)


def local(
    inputs,
    attn_out,
    out_grad,
    w_uvqk,
    w_output,
    norm_gain,
    rab_table,
    bucket_map,
    lengths,
    send_order,
    recv_order,
):
    key_value, query_grad, bias, gate, mixed, owned = pl.pallas_call(
        front_kernel,
        out_shape=(
            bf16(N_CTX, 128, 128),
            bf16(HALF, 128, 128),
            jax.ShapeDtypeStruct(((REACH + 1) * 128, 128), F32),
            bf16(ROWS, D),
            bf16(ROWS, D),
            bf16(ROWS, D),
        ),
        in_specs=in_vmem(10),
        out_specs=tuple(in_vmem(6)),
        scratch_shapes=[
            pltpu.VMEM((N_DP, 16, 128), BF16),
            pltpu.VMEM((N_DP, 16, 128), BF16),
            pltpu.VMEM((H, 128, 128), BF16),
            pltpu.VMEM((H, 128, 128), BF16),
            pltpu.SemaphoreType.DMA((3,)),
            pltpu.SemaphoreType.DMA((3,)),
        ],
        compiler_params=pltpu.CompilerParams(
            collective_id=0, has_side_effects=True, vmem_limit_bytes=LIMIT
        ),
    )(
        inputs,
        attn_out,
        out_grad,
        w_uvqk,
        w_output,
        norm_gain.reshape(1, D),
        rab_table,
        bucket_map.reshape(8, 128),
        send_order,
        recv_order,
    )
    grad_kv, grad_qt = pl.pallas_call(
        attend_kernel,
        out_shape=(bf16(TILES, 128, 128), bf16(HALF, 64, 128)),
        in_specs=[pl.BlockSpec(memory_space=pltpu.SMEM)] + in_vmem(3),
        out_specs=tuple(in_vmem(2)),
        scratch_shapes=[
            pltpu.VMEM(((TILES + REACH) * 128, 128), BF16),
            pltpu.VMEM((64, (TILES + REACH) * 128), BF16),
            pltpu.VMEM(((TILES + REACH) * 128, 128), F32),
            pltpu.VMEM((64, 128), F32),
        ],
        compiler_params=pltpu.CompilerParams(vmem_limit_bytes=LIMIT),
    )(lengths, key_value, query_grad, bias)
    return pl.pallas_call(
        back_kernel,
        out_shape=(bf16(ROWS, D), bf16(32, 64), bf16(32, 16)),
        in_specs=in_vmem(10),
        out_specs=tuple(in_vmem(3)),
        scratch_shapes=[
            pltpu.VMEM((N_CTX, 128, 128), BF16),
            pltpu.VMEM((HALF, 64, 128), BF16),
            pltpu.VMEM((N_DP, 16, 128), BF16),
            pltpu.VMEM((N_DP, 16, 128), BF16),
            pltpu.VMEM((ROWS, D), BF16),
            pltpu.VMEM((ROWS, D), BF16),
            pltpu.VMEM((ROWS, 256), BF16),
            pltpu.VMEM((ROWS, 1024), BF16),
            pltpu.VMEM((ROWS, 256), BF16),
            pltpu.VMEM((ROWS, 1024), BF16),
            pltpu.VMEM((N_CTX, 32, TERM_COLS), BF16),
            pltpu.VMEM((N_CTX, 32, TERM_COLS), BF16),
            pltpu.VMEM((N_Z, 32, 128), BF16),
            pltpu.VMEM((N_Z, 32, 128), BF16),
            pltpu.SemaphoreType.DMA((9,)),
            pltpu.SemaphoreType.DMA((9,)),
        ],
        compiler_params=pltpu.CompilerParams(
            collective_id=1, has_side_effects=True, vmem_limit_bytes=LIMIT
        ),
    )(
        inputs,
        out_grad,
        w_uvqk,
        send_order,
        recv_order,
        grad_kv,
        grad_qt,
        gate,
        mixed,
        owned,
    )


def solution(mesh):
    in_specs = (
        P(("dp", "ctx"), None),
        P(("dp", "ctx"), None),
        P(("dp", "ctx"), None),
        P(),
        P(),
        P(),
        P(),
        P(),
        P("dp", None),
        P(("dp", "ctx"), None),
        P(("dp", "ctx"), None),
    )
    out_specs = (P(("dp", "ctx"), None), P("ctx", "dp"), P("ctx", "dp"))
    return jax.shard_map(local, mesh=mesh, in_specs=in_specs, out_specs=out_specs, check_vma=False)
```

```python
import jax
import jax.numpy as jnp
from jax import lax
from jax.experimental import pallas as pl
from jax.experimental.pallas import tpu as pltpu
from jax.sharding import PartitionSpec as P

MESH = pl.DeviceIdType.MESH
F32 = jnp.float32
BF16 = jnp.bfloat16

D = 512
H = 8
ROWS = 128
N_DP = 32
N_CTX = 16
N_Z = 16
TILES = 16
REACH = 8
PAIRS = 8
HALF = 8
SLOTS = 512
EARLY = 512
LATE = 768
WINDOW = 5
EPS = 1e-05
LIMIT = 56 * 1024 * 1024


def mm(left, right, dims=((1,), (0,))):
    return lax.dot_general(left, right, (dims, ((), ())), preferred_element_type=F32)


def iota(shape, dim):
    return lax.broadcasted_iota(jnp.int32, shape, dim)


def slot_of(place):
    return (place >> 4) * 4 + (place & 3)


def piece_of(place):
    return (place >> 2) & 3


def sigmoid(array):
    return 1.0 / (1.0 + jnp.exp(-array))


def half_of(ctx):
    return lax.rem((ctx + 1) // 2, 2)


def member(index, half):
    return 2 * index + lax.rem(half + index, 2)


def by_piece(wide):
    piece = piece_of(iota((SLOTS, 128), 0))
    out = wide[:, :128]
    for part in range(1, 4):
        out = jnp.where(piece == part, wide[:, part * 128 : part * 128 + 128], out)
    return out


def pick_pieces(hot, flat):
    piece = piece_of(iota(hot.shape, 1))
    parts = [mm(jnp.where(piece == part, hot, 0.0).astype(BF16), flat) for part in range(4)]
    return jnp.concatenate(parts, axis=1)


def swap(array):
    return pltpu.roll(array, 64, 1)


def announce(me_dp, me_ctx):
    barrier = pltpu.get_barrier_semaphore()

    def tell_dp(step, carry):
        peer = lax.rem(me_dp + step, N_DP)
        pl.semaphore_signal(barrier, inc=1, device_id=(peer, me_ctx), device_id_type=MESH)
        return carry

    def tell_ctx(step, carry):
        peer = lax.rem(me_ctx + step, N_CTX)
        pl.semaphore_signal(barrier, inc=1, device_id=(me_dp, peer), device_id_type=MESH)
        return carry

    lax.fori_loop(1, N_DP, tell_dp, 0)
    lax.fori_loop(1, N_CTX, tell_ctx, 0)


def everyone_in():
    pl.semaphore_wait(pltpu.get_barrier_semaphore(), N_DP - 1 + N_CTX - 1)


def spread(count, copy_to):
    def one(step, carry):
        copy_to(step).start()
        return carry

    lax.fori_loop(1, count, one, 0)


def layer_kernel(
    len_ref,
    x_hbm,
    attn_hbm,
    og_hbm,
    w_hbm,
    wo_hbm,
    gain_hbm,
    rab_hbm,
    bm_hbm,
    so_hbm,
    ro_hbm,
    rows_out,
    uvqk_out,
    output_out,
    x_ref,
    attn_ref,
    og_ref,
    w_ref,
    wo_ref,
    gain_ref,
    rab_ref,
    bm_ref,
    so_ref,
    ro_ref,
    sorted_rows,
    arrived,
    kv_send,
    kv_got,
    qg_send,
    qg_got,
    bias,
    turned,
    pairs,
    dqt_total,
    dkv_send,
    dkv_got,
    dqt_send,
    dqt_got,
    slope_ref,
    back_rows,
    returned,
    mixed_send,
    early_send,
    late_send,
    other_x,
    other_mixed,
    other_early,
    other_late,
    x_turned,
    early_terms,
    early_got,
    late_terms,
    late_got,
    last_send,
    last_got,
    load_sem,
    send_sem,
    recv_sem,
):
    me_dp = lax.axis_index("dp")
    me_ctx = lax.axis_index("ctx")
    core = lax.rem(me_dp, 2)
    me_z = me_dp // 2
    half = half_of(me_ctx)
    own = me_ctx // 2
    partner = me_dp + 1 - 2 * core
    next_ctx = lax.rem(me_ctx + 1, N_CTX)
    next_dp = lax.rem(me_dp + 1, N_DP)

    def remote(source, target, number, dp, ctx):
        return pltpu.make_async_remote_copy(
            src_ref=source,
            dst_ref=target,
            send_sem=send_sem.at[number],
            recv_sem=recv_sem.at[number],
            device_id=(dp, ctx),
            device_id_type=MESH,
        )

    def many(source, target, number, count, dp, ctx):
        return remote(source.at[pl.ds(0, count)], target.at[pl.ds(0, count)], number, dp, ctx)

    loads = [
        pltpu.make_async_copy(source, target, load_sem.at[number])
        for number, (source, target) in enumerate(
            (
                (so_hbm, so_ref),
                (og_hbm, og_ref),
                (x_hbm, x_ref),
                (w_hbm, w_ref),
                (attn_hbm, attn_ref),
                (gain_hbm, gain_ref),
                (rab_hbm, rab_ref),
                (bm_hbm, bm_ref),
                (ro_hbm, ro_ref),
                (wo_hbm, wo_ref),
            )
        )
    ]
    for load in loads:
        load.start()
    announce(me_dp, me_ctx)
    low = iota((ROWS, 128), 1) < 64

    loads[0].wait()
    loads[1].wait()
    order = so_ref[...].astype(F32)
    lane = iota((SLOTS, 128), 1)
    place = iota((SLOTS, 128), 0)
    wanted = jnp.sum(jnp.where(lane == slot_of(place), order, 0.0), axis=1, keepdims=True)
    hot = jnp.where(lane.astype(F32) == wanted, 1.0, 0.0).astype(BF16)
    sorted_rows[...] = by_piece(mm(hot, og_ref[...])).astype(BF16).reshape(N_DP, 16, 128)
    arrived[me_dp] = sorted_rows[me_dp]
    loads[2].wait()
    everyone_in()

    def row_copy(step):
        peer = lax.rem(me_dp + step, N_DP)
        return remote(sorted_rows.at[peer], arrived.at[me_dp], 0, peer, me_ctx)

    spread(N_DP, row_copy)
    x_copy = remote(x_ref, other_x, 1, partner, me_ctx)
    x_copy.start()

    x = x_ref[...]
    loads[3].wait()
    pre_v = mm(x, w_ref[:, D : 2 * D])
    sig_v = sigmoid(pre_v)
    slope_ref[:, :D] = sig_v * (1.0 + pre_v * (1.0 - sig_v))
    value = pre_v * sig_v
    pre_k = mm(x, w_ref[:, 3 * D :])
    sig_k = sigmoid(pre_k)
    slope_ref[:, 2 * D :] = sig_k * (1.0 + pre_k * (1.0 - sig_k))
    key = pre_k * sig_k
    for pair in range(H // 2):
        k_two = key[:, pair * 128 : pair * 128 + 128]
        v_two = value[:, pair * 128 : pair * 128 + 128]
        kv_send[2 * pair] = jnp.where(low, k_two, swap(v_two)).astype(BF16)
        kv_send[2 * pair + 1] = jnp.where(low, swap(k_two), v_two).astype(BF16)
    kv_got[me_ctx] = kv_send[own]

    def kv_copy(step):
        peer = lax.rem(me_ctx + step, N_CTX)
        return remote(kv_send.at[peer // 2], kv_got.at[me_ctx], 2, me_dp, peer)

    spread(N_CTX, kv_copy)

    pre_u = mm(x, w_ref[:, :D])
    sig_u = sigmoid(pre_u)
    gating = (pre_u * sig_u).astype(BF16).astype(F32)
    slope_u = sig_u * (1.0 + pre_u * (1.0 - sig_u))
    pre_q = mm(x, w_ref[:, 2 * D : 3 * D])
    sig_q = sigmoid(pre_q)
    slope_ref[:, D : 2 * D] = sig_q * (1.0 + pre_q * (1.0 - sig_q))
    query = (pre_q * sig_q).astype(BF16).astype(F32) * 0.0625
    for load in loads[4:]:
        load.wait()
    gain = gain_ref[...]
    attn = attn_ref[...].astype(F32)
    centred = attn - jnp.mean(attn, axis=1, keepdims=True)
    inv_std = lax.rsqrt(jnp.mean(centred * centred, axis=1, keepdims=True) + EPS)
    normal_hat = centred * inv_std
    normed = normal_hat * gain
    mixed_send[...] = (normed * gating).astype(BF16)
    mixed_copy = remote(mixed_send, other_mixed, 3, partner, me_ctx)
    mixed_copy.start()
    gate_scale = normed * slope_u
    hat_scale = gating * gain

    buckets = iota((128, 128), 0)
    own_head = iota((H, 128), 0) == own
    lines = []
    for block in range(REACH):
        chosen = jnp.where(buckets == bm_ref[block : block + 1, :], 1.0, 0.0)
        table = lax.dot_general(
            rab_ref[...],
            chosen,
            (((1,), (0,)), ((), ())),
            precision=lax.Precision.HIGHEST,
            preferred_element_type=F32,
        )
        lines.append(jnp.sum(jnp.where(own_head, table, 0.0), axis=0, keepdims=True) * 0.5)
    blank = jnp.zeros((1, 128), F32)
    for far in range(REACH + 1):
        current = lines[far] if far < REACH else blank
        before = lines[far - 1] if far > 0 else blank
        both = jnp.broadcast_to(jnp.concatenate([current, before], axis=1), (128, 256))
        tile = pltpu.roll(both, 0, 1, stride=1, stride_axis=0)[:, :128]
        bias[(REACH + 1 - far) * 128 : (REACH + 2 - far) * 128, :] = tile
    bias[:128, :] = jnp.zeros((128, 128), F32)
    bias[(REACH + 2) * 128 :, :] = jnp.zeros((128, 128), F32)
    pairs[HALF:] = jnp.zeros((WINDOW - 1, 256, 128), BF16)
    dqt_total[...] = jnp.zeros(dqt_total.shape, F32)

    taken = ro_ref[...].astype(F32)
    square = iota((128, 128), 0) == iota((128, 128), 1)
    slot_col = jnp.sum(jnp.where(square, taken, 0.0), axis=1, keepdims=True)
    place = iota((ROWS, SLOTS), 1)
    hot = jnp.where(slot_of(place).astype(F32) == slot_col, 1.0, 0.0)
    column = iota((D, 256), 1)
    source_row = iota((D, 256), 0)
    spread_col = (column >> 4) * 32 + (column & 15)
    pick_own = jnp.where(source_row == spread_col + 16 * core, 1.0, 0.0).astype(BF16)
    pick_else = jnp.where(source_row == spread_col + 16 * (1 - core), 1.0, 0.0).astype(BF16)
    zero_core = jnp.broadcast_to(core, (ROWS, 128)) == 0

    def by_core(first, second):
        even = jnp.where(low, first, swap(second))
        odd = jnp.where(low, swap(first), second)
        return (
            jnp.where(zero_core, even, odd).astype(BF16),
            jnp.where(zero_core, odd, even).astype(BF16),
        )

    row_wait = many(sorted_rows, arrived, 0, N_DP - 1, next_dp, me_ctx)
    row_wait.wait_recv()
    owned = pick_pieces(hot, arrived[...].reshape(SLOTS, 128)).astype(BF16)
    grad_z = mm(owned, wo_ref[...], ((1,), (1,)))
    grad_hat = grad_z * hat_scale
    grad_attn = (
        grad_hat
        - jnp.mean(grad_hat, axis=1, keepdims=True)
        - normal_hat * jnp.mean(grad_hat * normal_hat, axis=1, keepdims=True)
    ) * inv_std
    for pair in range(H // 2):
        q_two = query[:, pair * 128 : pair * 128 + 128]
        g_two = grad_attn[:, pair * 128 : pair * 128 + 128]
        qg_send[2 * pair] = jnp.where(low, q_two, swap(g_two)).astype(BF16)
        qg_send[2 * pair + 1] = jnp.where(low, swap(q_two), g_two).astype(BF16)
    qg_got[own] = qg_send[own]

    def qg_copy(step):
        head = lax.rem(own + step, HALF)
        return remote(qg_send.at[head], qg_got.at[own], 4, me_dp, member(head, half))

    spread(HALF, qg_copy)

    gate = grad_z * gate_scale
    gate_own = []
    for block in range(2):
        first = gate[:, 256 * block : 256 * block + 128]
        second = gate[:, 256 * block + 128 : 256 * block + 256]
        kept, given = by_core(first, second)
        gate_own.append(kept)
        early_send[:, 128 * block : 128 * block + 128] = given
    early_send[:, 256:] = mm(owned, pick_else).astype(BF16)
    early_copy = remote(early_send, other_early, 5, partner, me_ctx)
    early_copy.start()
    gate_own = jnp.concatenate(gate_own, axis=1)
    owned_own = mm(owned, pick_own).astype(BF16)
    gate = gate.astype(BF16)

    kv_wait = many(kv_got, kv_got, 2, N_CTX - 1, me_dp, next_ctx)
    kv_wait.wait_recv()
    for tile in range(TILES):
        flipped = kv_got[tile].astype(F32).T
        turned[:, tile * 128 : tile * 128 + 128] = flipped[:64].astype(BF16)
    x_copy.wait_recv()
    x_turned[:, :ROWS] = x.astype(F32).T.astype(BF16)
    x_turned[:, ROWS:] = other_x[...].astype(F32).T.astype(BF16)
    mixed_copy.wait_recv()
    early_copy.wait_recv()
    gate_both = jnp.concatenate([gate_own, other_early[:, :256]], axis=0)
    owned_both = jnp.concatenate([owned_own, other_early[:, 256:]], axis=0)
    mixed_both = jnp.concatenate([mixed_send[...], other_mixed[...]], axis=0)
    first = mm(x_turned[...], gate_both).astype(BF16)
    early_terms[:, :, :256] = first.reshape(N_CTX, 32, 256)
    second = mm(mixed_both, owned_both, ((0,), (0,))).astype(BF16)
    early_terms[:, :, 256:] = second.reshape(N_CTX, 32, 256)
    early_got[me_ctx] = early_terms[me_ctx]

    def early_term_copy(step):
        peer = lax.rem(me_ctx + step, N_CTX)
        return remote(early_terms.at[peer], early_got.at[me_ctx], 6, me_dp, peer)

    spread(N_CTX, early_term_copy)

    qg_wait = many(qg_send, qg_got, 4, HALF - 1, me_dp, next_ctx)
    qg_wait.wait_recv()
    for index in range(HALF):
        block = qg_got[index].astype(F32)
        pairs[index] = jnp.concatenate(
            [jnp.where(low, block, 0.0), jnp.where(low, 0.0, block)], axis=0
        ).astype(BF16)
    edge_one = len_ref[0, 0]
    edge_two = edge_one + len_ref[0, 1]
    edge_three = edge_two + len_ref[0, 2]

    def meet(keys, keys_turned, pair_index, index):
        tile = member(index, half)
        place = tile * 128 + iota((1, 128), 1)
        first = jnp.where(place >= edge_one, edge_one, 0)
        first = jnp.where(place >= edge_two, edge_two, first)
        first = jnp.where(place >= edge_three, edge_three, first)
        both = mm(keys, pairs[index], ((1,), (1,)))
        row = pl.multiple_of((REACH + 1 - tile + 2 * pair_index) * 128, 128)
        scores = both[:, :128] + bias[pl.ds(row, 256), :]
        bent = jnp.tanh(scores)
        rise = 1.0 + bent
        weights = scores * rise
        slopes = both[:, 128:] * (rise + weights * (1.0 - bent))
        key_place = pair_index * 256 + iota((256, 128), 0)
        allowed = (key_place >= first) & (key_place <= place)
        weights = jnp.where(allowed, weights, 0.0).astype(BF16)
        slopes = jnp.where(allowed, slopes, 0.0).astype(BF16)
        dqt_total[index] += mm(keys_turned, slopes)
        return jnp.concatenate([slopes, weights], axis=1)

    def one_pair(step, carry):
        pair_index = lax.rem(own + 1 + step, PAIRS)
        keys = kv_got[pl.ds(2 * pair_index, 2)].reshape(256, 128)
        keys_turned = turned[:, pl.ds(pl.multiple_of(pair_index * 256, 256), 256)]
        found = [meet(keys, keys_turned, pair_index, pair_index + k) for k in range(WINDOW)]
        total = mm(
            jnp.concatenate(found, axis=1),
            pairs[pl.ds(pair_index, WINDOW)].reshape(WINDOW * 256, 128),
        )
        dkv_send[pl.ds(2 * pair_index, 2)] = (
            (total * (1.0 / 1024.0)).astype(BF16).reshape(2, 128, 128)
        )
        for side in range(2):
            peer = 2 * pair_index + side

            @pl.when(peer != me_ctx)
            def _():
                remote(dkv_send.at[peer], dkv_got.at[me_ctx], 7, me_dp, peer).start()

        return carry

    lax.fori_loop(0, PAIRS, one_pair, 0)
    dkv_got[me_ctx] = dkv_send[me_ctx]
    dqt_send[...] = (dqt_total[:HALF] * (1.0 / 16384.0)).astype(BF16)
    dqt_got[own] = dqt_send[own]

    def dqt_copy(step):
        index = lax.rem(own + step, HALF)
        return remote(dqt_send.at[index], dqt_got.at[own], 8, me_dp, member(index, half))

    spread(HALF, dqt_copy)

    slot = slot_of(iota((SLOTS, ROWS), 0))
    back_hot = jnp.where(slot == ro_ref[...], 1.0, 0.0).astype(BF16)
    sent = jnp.where(iota((ROWS, 128), 0) == so_ref[...], 1.0, 0.0).astype(BF16)
    place = iota((ROWS, SLOTS), 1)
    spot = jnp.where(iota((ROWS, SLOTS), 0) == slot_of(place), 1.0, 0.0).astype(BF16)
    final_hot = mm(sent, spot)

    dkv_wait = many(dkv_send, dkv_got, 7, N_CTX - 1, me_dp, next_ctx)
    dqt_wait = many(dqt_send, dqt_got, 8, HALF - 1, me_dp, next_ctx)
    dkv_wait.wait_recv()
    grad_k = []
    grad_v = []
    for pair in range(H // 2):
        even = dkv_got[4 * pair].astype(F32) + dkv_got[4 * pair + 1].astype(F32)
        odd = dkv_got[4 * pair + 2].astype(F32) + dkv_got[4 * pair + 3].astype(F32)
        grad_k.append(jnp.where(low, even, swap(odd)))
        grad_v.append(jnp.where(low, swap(even), odd))
    dqt_wait.wait_recv()
    grad_q = dqt_got[...].reshape(D, 128).astype(F32).T
    after = jnp.concatenate(grad_v + [grad_q] + grad_k, axis=1) * slope_ref[...]
    late_own = []
    for block in range(6):
        first = after[:, 256 * block : 256 * block + 128]
        second = after[:, 256 * block + 128 : 256 * block + 256]
        kept, given = by_core(first, second)
        late_own.append(kept)
        late_send[:, 128 * block : 128 * block + 128] = given
    late_copy = remote(late_send, other_late, 9, partner, me_ctx)
    late_copy.start()
    grad_pre = jnp.concatenate([gate, after.astype(BF16)], axis=1)
    branch = mm(grad_pre, w_ref[...], ((1,), (1,))).astype(BF16)
    back_rows[...] = by_piece(mm(back_hot, branch)).astype(BF16).reshape(N_DP, 16, 128)
    returned[me_dp] = back_rows[me_dp]

    def back_copy(step):
        peer = lax.rem(me_dp + step, N_DP)
        return remote(back_rows.at[peer], returned.at[me_dp], 10, peer, me_ctx)

    spread(N_DP, back_copy)

    late_copy.wait_recv()
    late_both = jnp.concatenate([jnp.concatenate(late_own, axis=1), other_late[...]], axis=0)
    late = mm(x_turned[...], late_both).astype(BF16)
    late_terms[...] = late.reshape(N_CTX, 32, LATE)
    late_got[me_ctx] = late_terms[me_ctx]

    def late_term_copy(step):
        peer = lax.rem(me_ctx + step, N_CTX)
        return remote(late_terms.at[peer], late_got.at[me_ctx], 11, me_dp, peer)

    spread(N_CTX, late_term_copy)

    early_wait = many(early_terms, early_got, 6, N_CTX - 1, me_dp, next_ctx)
    early_wait.wait_recv()
    early_sum = early_got[0].astype(F32)
    for source in range(1, N_CTX):
        early_sum = early_sum + early_got[source].astype(F32)

    back_wait = many(back_rows, returned, 10, N_DP - 1, next_dp, me_ctx)
    back_wait.wait_recv()
    arrival = pick_pieces(final_hot, returned[...].reshape(SLOTS, 128))
    rows_out[...] = (og_ref[...].astype(F32) + arrival).astype(BF16)

    late_wait = many(late_terms, late_got, 11, N_CTX - 1, me_dp, next_ctx)
    late_wait.wait_recv()
    late_sum = late_got[0].astype(F32)
    for source in range(1, N_CTX):
        late_sum = late_sum + late_got[source].astype(F32)

    low = iota((32, 128), 1) < 64
    for index in range(N_Z):
        if index < 4:
            block = early_sum[:, (index // 2) * 128 : (index // 2) * 128 + 128]
        else:
            block = late_sum[:, (index // 2 - 2) * 128 : (index // 2 - 1) * 128]
        if index % 2 == 1:
            block = swap(block)
        start = 256 + (index // 8) * 128
        extra = early_sum[:, start : start + 128]
        shift = (64 - 16 * (index % 8)) % 128
        if shift:
            extra = pltpu.roll(extra, shift, 1)
        last_send[index] = jnp.where(low, block, extra).astype(BF16)
    last_got[me_z] = last_send[me_z]

    def last_copy(step):
        peer = lax.rem(me_z + step, N_Z)
        return remote(last_send.at[peer], last_got.at[me_z], 12, 2 * peer + core, me_ctx)

    spread(N_Z, last_copy)
    last_wait = many(last_send, last_got, 12, N_Z - 1, 2 * lax.rem(me_z + 1, N_Z) + core, me_ctx)
    last_wait.wait_recv()
    total = last_got[0].astype(F32)
    for source in range(1, N_Z):
        total = total + last_got[source].astype(F32)
    total = (total * (1.0 / 256.0)).astype(BF16)
    uvqk_out[...] = total[:, :64]
    output_out[...] = total[:, 64:80]
    for copy in (
        row_wait,
        x_copy,
        kv_wait,
        mixed_copy,
        qg_wait,
        early_copy,
        early_wait,
        dkv_wait,
        dqt_wait,
        late_copy,
        back_wait,
        late_wait,
        last_wait,
    ):
        copy.wait_send()


def bf16(*shape):
    return jax.ShapeDtypeStruct(shape, BF16)


def local(
    inputs,
    attn_out,
    out_grad,
    w_uvqk,
    w_output,
    norm_gain,
    rab_table,
    bucket_map,
    lengths,
    send_order,
    recv_order,
):
    taken = (
        inputs,
        attn_out,
        out_grad,
        w_uvqk,
        w_output,
        norm_gain.reshape(1, D),
        rab_table,
        bucket_map.reshape(8, 128),
        send_order,
        recv_order,
    )
    vmem = pl.BlockSpec(memory_space=pltpu.VMEM)
    scratch = [pltpu.VMEM(array.shape, array.dtype) for array in taken]
    for shape, kind in (
        ((N_DP, 16, 128), BF16),
        ((N_DP, 16, 128), BF16),
        ((H, 128, 128), BF16),
        ((N_CTX, 128, 128), BF16),
        ((H, 128, 128), BF16),
        ((HALF, 128, 128), BF16),
        (((REACH + 3) * 128, 128), F32),
        ((64, TILES * 128), BF16),
        ((HALF + WINDOW - 1, 256, 128), BF16),
        ((HALF + WINDOW - 1, 64, 128), F32),
        ((N_CTX, 128, 128), BF16),
        ((N_CTX, 128, 128), BF16),
        ((HALF, 64, 128), BF16),
        ((HALF, 64, 128), BF16),
        ((ROWS, 3 * D), F32),
        ((N_DP, 16, 128), BF16),
        ((N_DP, 16, 128), BF16),
        ((ROWS, D), BF16),
        ((ROWS, EARLY), BF16),
        ((ROWS, LATE), BF16),
        ((ROWS, D), BF16),
        ((ROWS, D), BF16),
        ((ROWS, EARLY), BF16),
        ((ROWS, LATE), BF16),
        ((D, 2 * ROWS), BF16),
        ((N_CTX, 32, EARLY), BF16),
        ((N_CTX, 32, EARLY), BF16),
        ((N_CTX, 32, LATE), BF16),
        ((N_CTX, 32, LATE), BF16),
        ((N_Z, 32, 128), BF16),
        ((N_Z, 32, 128), BF16),
    ):
        scratch.append(pltpu.VMEM(shape, kind))
    scratch += [
        pltpu.SemaphoreType.DMA((10,)),
        pltpu.SemaphoreType.DMA((13,)),
        pltpu.SemaphoreType.DMA((13,)),
    ]
    return pl.pallas_call(
        layer_kernel,
        out_shape=(bf16(ROWS, D), bf16(32, 64), bf16(32, 16)),
        in_specs=[pl.BlockSpec(memory_space=pltpu.SMEM)]
        + [pl.BlockSpec(memory_space=pl.ANY)] * len(taken),
        out_specs=(vmem, vmem, vmem),
        scratch_shapes=scratch,
        compiler_params=pltpu.CompilerParams(
            collective_id=0, has_side_effects=True, vmem_limit_bytes=LIMIT
        ),
    )(lengths, *taken)


def solution(mesh):
    in_specs = (
        P(("dp", "ctx"), None),
        P(("dp", "ctx"), None),
        P(("dp", "ctx"), None),
        P(),
        P(),
        P(),
        P(),
        P(),
        P("dp", None),
        P(("dp", "ctx"), None),
        P(("dp", "ctx"), None),
    )
    out_specs = (P(("dp", "ctx"), None), P("ctx", "dp"), P("ctx", "dp"))
    return jax.shard_map(local, mesh=mesh, in_specs=in_specs, out_specs=out_specs, check_vma=False)
```

```python
import jax
import jax.numpy as jnp
from jax import lax
from jax.experimental import pallas as pl
from jax.experimental.pallas import tpu as pltpu
from jax.sharding import PartitionSpec as P

MESH = pl.DeviceIdType.MESH
F32 = jnp.float32
BF16 = jnp.bfloat16

D = 512
H = 8
ROWS = 128
N_DP = 32
N_CTX = 16
N_Z = 16
TILES = 16
REACH = 8
PAIRS = 8
HALF = 8
SLOTS = 512
EARLY = 512
LATE = 768
EPS = 1e-05
LIMIT = 56 * 1024 * 1024


def mm(left, right, dims=((1,), (0,))):
    return lax.dot_general(left, right, (dims, ((), ())), preferred_element_type=F32)


def iota(shape, dim):
    return lax.broadcasted_iota(jnp.int32, shape, dim)


def slot_of(place):
    return (place >> 4) * 4 + (place & 3)


def piece_of(place):
    return (place >> 2) & 3


def sigmoid(array):
    return 1.0 / (1.0 + jnp.exp(-array))


def half_of(ctx):
    return lax.rem((ctx + 1) // 2, 2)


def member(index, half):
    return 2 * index + lax.rem(half + index, 2)


def by_piece(wide):
    piece = piece_of(iota((SLOTS, 128), 0))
    out = wide[:, :128]
    for part in range(1, 4):
        out = jnp.where(piece == part, wide[:, part * 128 : part * 128 + 128], out)
    return out


def pick_pieces(hot, flat):
    piece = piece_of(iota(hot.shape, 1))
    parts = [mm(jnp.where(piece == part, hot, 0.0).astype(BF16), flat) for part in range(4)]
    return jnp.concatenate(parts, axis=1)


def swap(array):
    return pltpu.roll(array, 64, 1)


def announce(me_dp, me_ctx):
    barrier = pltpu.get_barrier_semaphore()

    def tell_dp(step, carry):
        peer = lax.rem(me_dp + step, N_DP)
        pl.semaphore_signal(barrier, inc=1, device_id=(peer, me_ctx), device_id_type=MESH)
        return carry

    def tell_ctx(step, carry):
        peer = lax.rem(me_ctx + step, N_CTX)
        pl.semaphore_signal(barrier, inc=1, device_id=(me_dp, peer), device_id_type=MESH)
        return carry

    lax.fori_loop(1, N_DP, tell_dp, 0)
    lax.fori_loop(1, N_CTX, tell_ctx, 0)


def everyone_in():
    pl.semaphore_wait(pltpu.get_barrier_semaphore(), N_DP - 1 + N_CTX - 1)


def far_first(turn):
    return 8 + jnp.where(lax.rem(turn, 2) == 0, turn // 2, -((turn + 1) // 2))


def far_dp(me_dp, step):
    turn = step - 1
    peer_z = lax.rem(me_dp // 2 + far_first(turn // 2), N_Z)
    return 2 * peer_z + lax.rem(me_dp + 1 + turn, 2)


def spread(count, copy_to):
    def one(step, carry):
        copy_to(step).start()
        return carry

    lax.fori_loop(1, count, one, 0)


def layer_kernel(
    len_ref,
    x_hbm,
    attn_hbm,
    og_hbm,
    w_hbm,
    wo_hbm,
    gain_hbm,
    rab_hbm,
    bm_hbm,
    so_hbm,
    ro_hbm,
    rows_hbm,
    uvqk_hbm,
    output_hbm,
    x_ref,
    attn_ref,
    og_ref,
    w_ref,
    wo_ref,
    gain_ref,
    rab_ref,
    bm_ref,
    so_ref,
    ro_ref,
    sorted_rows,
    arrived,
    kv_send,
    kv_got,
    qg_send,
    qg_got,
    bias,
    turned,
    pairs,
    dqt_total,
    dkv_total,
    dkv_send,
    dkv_got,
    dqt_send,
    dqt_got,
    slope_ref,
    back_rows,
    returned,
    mixed_send,
    early_send,
    late_send,
    other_x,
    other_mixed,
    other_early,
    other_late,
    x_turned,
    mixed_turned,
    early_terms,
    early_got,
    late_terms,
    late_got,
    last_send,
    last_got,
    rows_out,
    uvqk_out,
    output_out,
    load_sem,
    send_sem,
    recv_sem,
):
    me_dp = lax.axis_index("dp")
    me_ctx = lax.axis_index("ctx")
    core = lax.rem(me_dp, 2)
    me_z = me_dp // 2
    half = half_of(me_ctx)
    own = me_ctx // 2
    partner = me_dp + 1 - 2 * core
    next_ctx = lax.rem(me_ctx + 1, N_CTX)
    next_dp = lax.rem(me_dp + 1, N_DP)

    def remote(source, target, number, dp, ctx):
        return pltpu.make_async_remote_copy(
            src_ref=source,
            dst_ref=target,
            send_sem=send_sem.at[number],
            recv_sem=recv_sem.at[number],
            device_id=(dp, ctx),
            device_id_type=MESH,
        )

    def many(source, target, number, count, dp, ctx):
        return remote(source.at[pl.ds(0, count)], target.at[pl.ds(0, count)], number, dp, ctx)

    loads = [
        pltpu.make_async_copy(source, target, load_sem.at[number])
        for number, (source, target) in enumerate(
            (
                (so_hbm, so_ref),
                (og_hbm, og_ref),
                (x_hbm, x_ref),
                (w_hbm, w_ref),
                (attn_hbm, attn_ref),
                (gain_hbm, gain_ref),
                (rab_hbm, rab_ref),
                (bm_hbm, bm_ref),
                (ro_hbm, ro_ref),
                (wo_hbm, wo_ref),
            )
        )
    ]
    for load in loads:
        load.start()
    announce(me_dp, me_ctx)
    low = iota((ROWS, 128), 1) < 64

    loads[0].wait()
    loads[1].wait()
    order = so_ref[...].astype(F32)
    lane = iota((SLOTS, 128), 1)
    place = iota((SLOTS, 128), 0)
    wanted = jnp.sum(jnp.where(lane == slot_of(place), order, 0.0), axis=1, keepdims=True)
    hot = jnp.where(lane.astype(F32) == wanted, 1.0, 0.0).astype(BF16)
    sorted_rows[...] = by_piece(mm(hot, og_ref[...])).astype(BF16).reshape(N_DP, 16, 128)
    arrived[me_dp] = sorted_rows[me_dp]
    loads[2].wait()
    everyone_in()

    def row_copy(step):
        peer = far_dp(me_dp, step)
        return remote(sorted_rows.at[peer], arrived.at[me_dp], 0, peer, me_ctx)

    spread(N_DP, row_copy)
    x_copy = remote(x_ref, other_x, 1, partner, me_ctx)
    x_copy.start()

    x = x_ref[...]
    loads[3].wait()
    pre_v = mm(x, w_ref[:, D : 2 * D])
    sig_v = sigmoid(pre_v)
    slope_ref[:, :D] = sig_v * (1.0 + pre_v * (1.0 - sig_v))
    value = pre_v * sig_v
    pre_k = mm(x, w_ref[:, 3 * D :])
    sig_k = sigmoid(pre_k)
    slope_ref[:, 2 * D :] = sig_k * (1.0 + pre_k * (1.0 - sig_k))
    key = pre_k * sig_k
    for pair in range(H // 2):
        k_two = key[:, pair * 128 : pair * 128 + 128]
        v_two = value[:, pair * 128 : pair * 128 + 128]
        kv_send[2 * pair] = jnp.where(low, k_two, swap(v_two)).astype(BF16)
        kv_send[2 * pair + 1] = jnp.where(low, swap(k_two), v_two).astype(BF16)
    kv_got[me_ctx] = kv_send[own]

    def kv_copy(step):
        peer = lax.rem(me_ctx + step, N_CTX)
        return remote(kv_send.at[peer // 2], kv_got.at[me_ctx], 2, me_dp, peer)

    spread(N_CTX, kv_copy)

    pre_u = mm(x, w_ref[:, :D])
    sig_u = sigmoid(pre_u)
    gating = (pre_u * sig_u).astype(BF16).astype(F32)
    slope_u = sig_u * (1.0 + pre_u * (1.0 - sig_u))
    pre_q = mm(x, w_ref[:, 2 * D : 3 * D])
    sig_q = sigmoid(pre_q)
    slope_ref[:, D : 2 * D] = sig_q * (1.0 + pre_q * (1.0 - sig_q))
    query = (pre_q * sig_q).astype(BF16).astype(F32) * 0.0625
    for load in loads[4:]:
        load.wait()
    gain = gain_ref[...]
    attn = attn_ref[...].astype(F32)
    centred = attn - jnp.mean(attn, axis=1, keepdims=True)
    inv_std = lax.rsqrt(jnp.mean(centred * centred, axis=1, keepdims=True) + EPS)
    normal_hat = centred * inv_std
    normed = normal_hat * gain
    mixed_send[...] = (normed * gating).astype(BF16)
    mixed_copy = remote(mixed_send, other_mixed, 3, partner, me_ctx)
    mixed_copy.start()
    gate_scale = normed * slope_u
    hat_scale = gating * gain

    buckets = iota((128, 128), 0)
    own_head = iota((H, 128), 0) == own
    lines = []
    for block in range(REACH):
        chosen = jnp.where(buckets == bm_ref[block : block + 1, :], 1.0, 0.0)
        table = lax.dot_general(
            rab_ref[...],
            chosen,
            (((1,), (0,)), ((), ())),
            precision=lax.Precision.HIGHEST,
            preferred_element_type=F32,
        )
        lines.append(jnp.sum(jnp.where(own_head, table, 0.0), axis=0, keepdims=True) * 0.5)
    blank = jnp.zeros((1, 128), F32)
    for far in range(REACH + 1):
        current = lines[far] if far < REACH else blank
        before = lines[far - 1] if far > 0 else blank
        both = jnp.broadcast_to(jnp.concatenate([current, before], axis=1), (128, 256))
        tile = pltpu.roll(both, 0, 1, stride=1, stride_axis=0)[:, :128]
        bias[(REACH + 1 - far) * 128 : (REACH + 2 - far) * 128, :] = tile
    bias[:128, :] = jnp.zeros((128, 128), F32)
    bias[(REACH + 2) * 128 :, :] = jnp.zeros((128, 128), F32)
    dqt_total[...] = jnp.zeros(dqt_total.shape, F32)

    taken = ro_ref[...].astype(F32)
    square = iota((128, 128), 0) == iota((128, 128), 1)
    slot_col = jnp.sum(jnp.where(square, taken, 0.0), axis=1, keepdims=True)
    place = iota((ROWS, SLOTS), 1)
    hot = jnp.where(slot_of(place).astype(F32) == slot_col, 1.0, 0.0)
    column = iota((D, 256), 1)
    source_row = iota((D, 256), 0)
    spread_col = (column >> 4) * 32 + (column & 15)
    pick_own = jnp.where(source_row == spread_col + 16 * core, 1.0, 0.0).astype(BF16)
    pick_else = jnp.where(source_row == spread_col + 16 * (1 - core), 1.0, 0.0).astype(BF16)
    zero_core = jnp.broadcast_to(core, (ROWS, 128)) == 0

    def by_core(first, second):
        even = jnp.where(low, first, swap(second))
        odd = jnp.where(low, swap(first), second)
        return (
            jnp.where(zero_core, even, odd).astype(BF16),
            jnp.where(zero_core, odd, even).astype(BF16),
        )

    x_turned[:, :ROWS] = x.astype(F32).T.astype(BF16)
    kv_wait = many(kv_got, kv_got, 2, N_CTX - 1, me_dp, next_ctx)
    kv_wait.wait_recv()
    for tile in range(TILES):
        flipped = kv_got[tile].astype(F32).T
        turned[:, tile * 128 : tile * 128 + 128] = flipped[:64].astype(BF16)
    x_copy.wait_recv()
    x_turned[:, ROWS:] = other_x[...].astype(F32).T.astype(BF16)
    mixed_copy.wait_recv()
    mixed_turned[:, :ROWS] = mixed_send[...].astype(F32).T.astype(BF16)
    mixed_turned[:, ROWS:] = other_mixed[...].astype(F32).T.astype(BF16)
    row_wait = many(sorted_rows, arrived, 0, N_DP - 1, next_dp, me_ctx)
    row_wait.wait_recv()
    owned = pick_pieces(hot, arrived[...].reshape(SLOTS, 128)).astype(BF16)
    grad_z = mm(owned, wo_ref[...], ((1,), (1,)))
    grad_hat = grad_z * hat_scale
    grad_attn = (
        grad_hat
        - jnp.mean(grad_hat, axis=1, keepdims=True)
        - normal_hat * jnp.mean(grad_hat * normal_hat, axis=1, keepdims=True)
    ) * inv_std
    for pair in range(H // 2):
        q_two = query[:, pair * 128 : pair * 128 + 128]
        g_two = grad_attn[:, pair * 128 : pair * 128 + 128]
        qg_send[2 * pair] = jnp.where(low, q_two, swap(g_two)).astype(BF16)
        qg_send[2 * pair + 1] = jnp.where(low, swap(q_two), g_two).astype(BF16)
    qg_got[own] = qg_send[own]

    def qg_copy(step):
        head = lax.rem(own + step, HALF)
        return remote(qg_send.at[head], qg_got.at[own], 4, me_dp, member(head, half))

    spread(HALF, qg_copy)

    gate = grad_z * gate_scale
    gate_own = []
    for block in range(2):
        first = gate[:, 256 * block : 256 * block + 128]
        second = gate[:, 256 * block + 128 : 256 * block + 256]
        kept, given = by_core(first, second)
        gate_own.append(kept)
        early_send[:, 128 * block : 128 * block + 128] = given
    early_send[:, 256:] = mm(owned, pick_else).astype(BF16)
    early_copy = remote(early_send, other_early, 5, partner, me_ctx)
    early_copy.start()
    gate_own = jnp.concatenate(gate_own, axis=1)
    owned_own = mm(owned, pick_own).astype(BF16)
    gate = gate.astype(BF16)

    early_copy.wait_recv()
    gate_both = jnp.concatenate([gate_own, other_early[:, :256]], axis=0)
    owned_both = jnp.concatenate([owned_own, other_early[:, 256:]], axis=0)
    first = mm(x_turned[...], gate_both).astype(BF16)
    early_terms[:, :, :256] = first.reshape(N_CTX, 32, 256)
    second = mm(mixed_turned[...], owned_both).astype(BF16)
    early_terms[:, :, 256:] = second.reshape(N_CTX, 32, 256)
    early_got[me_ctx] = early_terms[me_ctx]

    def early_term_copy(step):
        peer = lax.rem(me_ctx + step, N_CTX)
        return remote(early_terms.at[peer], early_got.at[me_ctx], 6, me_dp, peer)

    spread(N_CTX, early_term_copy)

    qg_wait = many(qg_send, qg_got, 4, HALF - 1, me_dp, next_ctx)
    qg_wait.wait_recv()
    for index in range(HALF):
        block = qg_got[index].astype(F32)
        pairs[index] = jnp.concatenate(
            [jnp.where(low, block, 0.0), jnp.where(low, 0.0, block)], axis=0
        ).astype(BF16)
    edge_one = len_ref[0, 0]
    edge_two = edge_one + len_ref[0, 1]
    edge_three = edge_two + len_ref[0, 2]

    dkv_total[...] = jnp.zeros(dkv_total.shape, F32)

    def meet(pair_index, index):
        keys = kv_got[pl.ds(2 * pair_index, 2)].reshape(256, 128)
        keys_turned = turned[:, pl.ds(pl.multiple_of(pair_index * 256, 256), 256)]
        tile = member(index, half)
        place = tile * 128 + iota((1, 128), 1)
        first = jnp.where(place >= edge_one, edge_one, 0)
        first = jnp.where(place >= edge_two, edge_two, first)
        first = jnp.where(place >= edge_three, edge_three, first)
        both = mm(keys, pairs[index], ((1,), (1,)))
        row = pl.multiple_of((REACH + 1 - tile + 2 * pair_index) * 128, 128)
        scores = both[:, :128] + bias[pl.ds(row, 256), :]
        bent = jnp.tanh(scores)
        key_place = pair_index * 256 + iota((256, 128), 0)
        allowed = (key_place >= first) & (key_place <= place)
        rise = jnp.where(allowed, 1.0 + bent, 0.0)
        weights = scores * rise
        slopes = (both[:, 128:] * (rise + weights * (1.0 - bent))).astype(BF16)
        dqt_total[index] += mm(keys_turned, slopes)
        found = jnp.concatenate([slopes, weights.astype(BF16)], axis=1)
        dkv_total[pair_index] += mm(found, pairs[index])

    def ship(pair_index):
        done = dkv_total[pair_index] * (1.0 / 1024.0)
        dkv_send[pl.ds(2 * pair_index, 2)] = done.astype(BF16).reshape(2, 128, 128)
        for side in range(2):
            peer = 2 * pair_index + side

            @pl.when(peer != me_ctx)
            def _():
                remote(dkv_send.at[peer], dkv_got.at[me_ctx], 7, me_dp, peer).start()

    def one_round(step, carry):
        turn = lax.rem(own + 1 + step, 6)
        for lag in range(3):
            meet(turn, turn + lag)
        meet(jnp.where(turn < 5, turn, 6), jnp.where(turn < 5, turn + 3, 6))
        meet(jnp.where(turn < 4, turn, 11 - turn), jnp.where(turn < 4, turn + 4, 7))
        ship(turn)

        @pl.when(turn >= 4)
        def _():
            ship(11 - turn)

        return carry

    lax.fori_loop(0, 6, one_round, 0)
    dkv_got[me_ctx] = dkv_send[me_ctx]
    dqt_send[...] = (dqt_total[...] * (1.0 / 16384.0)).astype(BF16)
    dqt_got[own] = dqt_send[own]

    def dqt_copy(step):
        index = lax.rem(own + step, HALF)
        return remote(dqt_send.at[index], dqt_got.at[own], 8, me_dp, member(index, half))

    spread(HALF, dqt_copy)

    slot = slot_of(iota((SLOTS, ROWS), 0))
    back_hot = jnp.where(slot == ro_ref[...], 1.0, 0.0).astype(BF16)
    sent = jnp.where(iota((ROWS, 128), 0) == so_ref[...], 1.0, 0.0).astype(BF16)
    place = iota((ROWS, SLOTS), 1)
    spot = jnp.where(iota((ROWS, SLOTS), 0) == slot_of(place), 1.0, 0.0).astype(BF16)
    final_hot = mm(sent, spot)

    dkv_wait = many(dkv_send, dkv_got, 7, N_CTX - 1, me_dp, next_ctx)
    dqt_wait = many(dqt_send, dqt_got, 8, HALF - 1, me_dp, next_ctx)
    dkv_wait.wait_recv()
    grad_k = []
    grad_v = []
    for pair in range(H // 2):
        even = dkv_got[4 * pair].astype(F32) + dkv_got[4 * pair + 1].astype(F32)
        odd = dkv_got[4 * pair + 2].astype(F32) + dkv_got[4 * pair + 3].astype(F32)
        grad_k.append(jnp.where(low, even, swap(odd)))
        grad_v.append(jnp.where(low, swap(even), odd))
    dqt_wait.wait_recv()
    grad_q = dqt_got[...].reshape(D, 128).astype(F32).T
    after = jnp.concatenate(grad_v + [grad_q] + grad_k, axis=1) * slope_ref[...]
    late_own = []
    for block in range(6):
        first = after[:, 256 * block : 256 * block + 128]
        second = after[:, 256 * block + 128 : 256 * block + 256]
        kept, given = by_core(first, second)
        late_own.append(kept)
        late_send[:, 128 * block : 128 * block + 128] = given
    late_copy = remote(late_send, other_late, 9, partner, me_ctx)
    late_copy.start()
    late_copy.wait_recv()
    late_both = jnp.concatenate([jnp.concatenate(late_own, axis=1), other_late[...]], axis=0)
    late = mm(x_turned[...], late_both).astype(BF16)
    late_terms[...] = late.reshape(N_CTX, 32, LATE)
    late_got[me_ctx] = late_terms[me_ctx]

    def late_term_copy(step):
        peer = lax.rem(me_ctx + step, N_CTX)
        return remote(late_terms.at[peer], late_got.at[me_ctx], 11, me_dp, peer)

    spread(N_CTX, late_term_copy)

    grad_pre = jnp.concatenate([gate, after.astype(BF16)], axis=1)
    branch = mm(grad_pre, w_ref[...], ((1,), (1,))).astype(BF16)
    back_rows[...] = by_piece(mm(back_hot, branch)).astype(BF16).reshape(N_DP, 16, 128)
    returned[me_dp] = back_rows[me_dp]

    def back_copy(step):
        peer = far_dp(me_dp, step)
        return remote(back_rows.at[peer], returned.at[me_dp], 10, peer, me_ctx)

    spread(N_DP, back_copy)

    early_wait = many(early_terms, early_got, 6, N_CTX - 1, me_dp, next_ctx)
    early_wait.wait_recv()
    early_sum = early_got[0].astype(F32)
    for source in range(1, N_CTX):
        early_sum = early_sum + early_got[source].astype(F32)

    back_wait = many(back_rows, returned, 10, N_DP - 1, next_dp, me_ctx)
    back_wait.wait_recv()
    arrival = pick_pieces(final_hot, returned[...].reshape(SLOTS, 128))
    rows_out[...] = (og_ref[...].astype(F32) + arrival).astype(BF16)
    rows_copy = pltpu.make_async_copy(rows_out, rows_hbm, load_sem.at[0])
    rows_copy.start()

    late_wait = many(late_terms, late_got, 11, N_CTX - 1, me_dp, next_ctx)
    late_wait.wait_recv()
    late_sum = late_got[0].astype(F32)
    for source in range(1, N_CTX):
        late_sum = late_sum + late_got[source].astype(F32)

    low = iota((32, 128), 1) < 64
    for index in range(N_Z):
        if index < 4:
            block = early_sum[:, (index // 2) * 128 : (index // 2) * 128 + 128]
        else:
            block = late_sum[:, (index // 2 - 2) * 128 : (index // 2 - 1) * 128]
        if index % 2 == 1:
            block = swap(block)
        start = 256 + (index // 8) * 128
        extra = early_sum[:, start : start + 128]
        shift = (64 - 16 * (index % 8)) % 128
        if shift:
            extra = pltpu.roll(extra, shift, 1)
        last_send[index] = jnp.where(low, block, extra).astype(BF16)
    last_got[me_z] = last_send[me_z]

    def last_copy(step):
        peer = lax.rem(me_z + far_first(step - 1), N_Z)
        return remote(last_send.at[peer], last_got.at[me_z], 12, 2 * peer + core, me_ctx)

    spread(N_Z, last_copy)
    last_wait = many(last_send, last_got, 12, N_Z - 1, 2 * lax.rem(me_z + 1, N_Z) + core, me_ctx)
    last_wait.wait_recv()
    total = last_got[0].astype(F32)
    for source in range(1, N_Z):
        total = total + last_got[source].astype(F32)
    total = total * (1.0 / 256.0)
    uvqk_out[...] = total[:, :64].astype(BF16)
    output_out[...] = total.T[64:80].astype(BF16)
    uvqk_copy = pltpu.make_async_copy(uvqk_out, uvqk_hbm, load_sem.at[1])
    output_copy = pltpu.make_async_copy(output_out, output_hbm, load_sem.at[2])
    uvqk_copy.start()
    output_copy.start()
    for copy in (
        row_wait,
        x_copy,
        kv_wait,
        mixed_copy,
        qg_wait,
        early_copy,
        early_wait,
        dkv_wait,
        dqt_wait,
        late_copy,
        back_wait,
        late_wait,
        last_wait,
    ):
        copy.wait_send()
    rows_copy.wait()
    uvqk_copy.wait()
    output_copy.wait()


def finish_kernel(rows, uvqk, output, rows_out, uvqk_out, output_out, *scratch):
    held, sems = scratch[:3], scratch[3]
    taken = [
        pltpu.make_async_copy(source, target, sems.at[number])
        for number, (source, target) in enumerate(zip((rows, uvqk, output), held))
    ]
    given = [
        pltpu.make_async_copy(source, target, sems.at[3 + number])
        for number, (source, target) in enumerate(zip(held, (rows_out, uvqk_out, output_out)))
    ]
    for copy in taken:
        copy.start()
    for first, second in zip(taken, given):
        first.wait()
        second.start()
    for copy in given:
        copy.wait()


def bf16(*shape):
    return jax.ShapeDtypeStruct(shape, BF16)


def local(
    inputs,
    attn_out,
    out_grad,
    w_uvqk,
    w_output,
    norm_gain,
    rab_table,
    bucket_map,
    lengths,
    send_order,
    recv_order,
):
    taken = (
        inputs,
        attn_out,
        out_grad,
        w_uvqk,
        w_output,
        norm_gain.reshape(1, D),
        rab_table,
        bucket_map.reshape(8, 128),
        send_order,
        recv_order,
    )
    anywhere = pl.BlockSpec(memory_space=pl.ANY)
    scratch = [pltpu.VMEM(array.shape, array.dtype) for array in taken]
    for shape, kind in (
        ((N_DP, 16, 128), BF16),
        ((N_DP, 16, 128), BF16),
        ((H, 128, 128), BF16),
        ((N_CTX, 128, 128), BF16),
        ((H, 128, 128), BF16),
        ((HALF, 128, 128), BF16),
        (((REACH + 3) * 128, 128), F32),
        ((64, TILES * 128), BF16),
        ((HALF, 256, 128), BF16),
        ((HALF, 64, 128), F32),
        ((PAIRS, 256, 128), F32),
        ((N_CTX, 128, 128), BF16),
        ((N_CTX, 128, 128), BF16),
        ((HALF, 64, 128), BF16),
        ((HALF, 64, 128), BF16),
        ((ROWS, 3 * D), F32),
        ((N_DP, 16, 128), BF16),
        ((N_DP, 16, 128), BF16),
        ((ROWS, D), BF16),
        ((ROWS, EARLY), BF16),
        ((ROWS, LATE), BF16),
        ((ROWS, D), BF16),
        ((ROWS, D), BF16),
        ((ROWS, EARLY), BF16),
        ((ROWS, LATE), BF16),
        ((D, 2 * ROWS), BF16),
        ((D, 2 * ROWS), BF16),
        ((N_CTX, 32, EARLY), BF16),
        ((N_CTX, 32, EARLY), BF16),
        ((N_CTX, 32, LATE), BF16),
        ((N_CTX, 32, LATE), BF16),
        ((N_Z, 32, 128), BF16),
        ((N_Z, 32, 128), BF16),
        ((ROWS, D), BF16),
        ((32, 64), BF16),
        ((16, 32), BF16),
    ):
        scratch.append(pltpu.VMEM(shape, kind))
    scratch += [
        pltpu.SemaphoreType.DMA((10,)),
        pltpu.SemaphoreType.DMA((13,)),
        pltpu.SemaphoreType.DMA((13,)),
    ]
    shapes = (bf16(ROWS, D), bf16(32, 64), bf16(16, 32))
    results = pl.pallas_call(
        layer_kernel,
        out_shape=shapes,
        in_specs=[pl.BlockSpec(memory_space=pltpu.SMEM)]
        + [anywhere] * len(taken),
        out_specs=(anywhere,) * 3,
        scratch_shapes=scratch,
        compiler_params=pltpu.CompilerParams(
            collective_id=0, has_side_effects=True, vmem_limit_bytes=LIMIT
        ),
    )(lengths, *taken)
    rows, uvqk, output = pl.pallas_call(
        finish_kernel,
        out_shape=shapes,
        in_specs=[anywhere] * 3,
        out_specs=(anywhere,) * 3,
        scratch_shapes=[pltpu.VMEM(shape.shape, shape.dtype) for shape in shapes]
        + [pltpu.SemaphoreType.DMA((6,))],
        compiler_params=pltpu.CompilerParams(vmem_limit_bytes=LIMIT),
    )(*results)
    return rows, uvqk, output.T


def solution(mesh):
    in_specs = (
        P(("dp", "ctx"), None),
        P(("dp", "ctx"), None),
        P(("dp", "ctx"), None),
        P(),
        P(),
        P(),
        P(),
        P(),
        P("dp", None),
        P(("dp", "ctx"), None),
        P(("dp", "ctx"), None),
    )
    out_specs = (P(("dp", "ctx"), None), P("ctx", "dp"), P("ctx", "dp"))
    return jax.shard_map(local, mesh=mesh, in_specs=in_specs, out_specs=out_specs, check_vma=False)
```

```python
import jax
import jax.numpy as jnp
from jax import lax
from jax.experimental import pallas as pl
from jax.experimental.pallas import tpu as pltpu
from jax.sharding import PartitionSpec as P

MESH = pl.DeviceIdType.MESH
F32 = jnp.float32
BF16 = jnp.bfloat16

D = 512
H = 8
ROWS = 128
N_DP = 32
N_CTX = 16
N_Z = 16
TILES = 16
REACH = 8
PAIRS = 8
HALF = 8
SLOTS = 512
EARLY = 512
LATE = 768
EPS = 1e-05
LIMIT = 56 * 1024 * 1024


def mm(left, right, dims=((1,), (0,))):
    return lax.dot_general(left, right, (dims, ((), ())), preferred_element_type=F32)


def iota(shape, dim):
    return lax.broadcasted_iota(jnp.int32, shape, dim)


def slot_of(place):
    return (place >> 4) * 4 + (place & 3)


def piece_of(place):
    return (place >> 2) & 3


def sigmoid(array):
    return 1.0 / (1.0 + jnp.exp(-array))


def half_of(ctx):
    return lax.rem((ctx + 1) // 2, 2)


def member(index, half):
    return 2 * index + lax.rem(half + index, 2)


def by_piece(wide):
    piece = piece_of(iota((SLOTS, 128), 0))
    out = wide[:, :128]
    for part in range(1, 4):
        out = jnp.where(piece == part, wide[:, part * 128 : part * 128 + 128], out)
    return out


def pick_pieces(hot, flat):
    piece = piece_of(iota(hot.shape, 1))
    parts = [mm(jnp.where(piece == part, hot, 0.0).astype(BF16), flat) for part in range(4)]
    return jnp.concatenate(parts, axis=1)


def swap(array):
    return pltpu.roll(array, 64, 1)


def far_first(turn):
    return 8 + jnp.where(lax.rem(turn, 2) == 0, turn // 2, -((turn + 1) // 2))


def far_dp(me_dp, step):
    turn = step - 1
    peer_z = lax.rem(me_dp // 2 + far_first(turn // 2), N_Z)
    return 2 * peer_z + lax.rem(me_dp + 1 + turn, 2)


def announce(me_dp, me_ctx):
    barrier = pltpu.get_barrier_semaphore()

    def tell_dp(step, carry):
        peer = far_dp(me_dp, step)
        pl.semaphore_signal(barrier, inc=1, device_id=(peer, me_ctx), device_id_type=MESH)
        return carry

    def tell_ctx(step, carry):
        peer = lax.rem(me_ctx + step, N_CTX)
        pl.semaphore_signal(barrier, inc=1, device_id=(me_dp, peer), device_id_type=MESH)
        return carry

    lax.fori_loop(1, N_DP, tell_dp, 0)
    lax.fori_loop(1, N_CTX, tell_ctx, 0)


def everyone_in():
    pl.semaphore_wait(pltpu.get_barrier_semaphore(), N_DP - 1 + N_CTX - 1)


def spread(count, copy_to):
    def one(step, carry):
        copy_to(step).start()
        return carry

    lax.fori_loop(1, count, one, 0)


def layer_kernel(
    len_ref,
    x_hbm,
    attn_hbm,
    og_hbm,
    w_hbm,
    wo_hbm,
    gain_hbm,
    rab_hbm,
    bm_hbm,
    so_hbm,
    ro_hbm,
    rows_hbm,
    uvqk_hbm,
    output_hbm,
    x_ref,
    attn_ref,
    og_ref,
    w_ref,
    wo_ref,
    gain_ref,
    rab_ref,
    bm_ref,
    so_ref,
    ro_ref,
    sorted_rows,
    arrived,
    kv_send,
    kv_got,
    q_send,
    q_got,
    g_send,
    g_got,
    bias,
    turned,
    pairs,
    dqt_total,
    dkv_total,
    dkv_send,
    dkv_got,
    dqt_send,
    dqt_got,
    slope_ref,
    back_rows,
    returned,
    mixed_send,
    early_send,
    late_send,
    other_x,
    other_mixed,
    other_early,
    other_late,
    x_turned,
    mixed_turned,
    early_terms,
    early_got,
    early_spread,
    early_parts,
    late_x,
    late_y,
    late_gx,
    late_gy,
    late_mx,
    late_my,
    late_ex,
    late_ey,
    last_send,
    last_got,
    rows_out,
    uvqk_out,
    output_out,
    load_sem,
    send_sem,
    recv_sem,
):
    me_dp = lax.axis_index("dp")
    me_ctx = lax.axis_index("ctx")
    core = lax.rem(me_dp, 2)
    me_z = me_dp // 2
    half = half_of(me_ctx)
    own = me_ctx // 2
    partner = me_dp + 1 - 2 * core
    next_ctx = lax.rem(me_ctx + 1, N_CTX)
    next_dp = lax.rem(me_dp + 1, N_DP)

    announce(me_dp, me_ctx)

    def remote(source, target, number, dp, ctx):
        return pltpu.make_async_remote_copy(
            src_ref=source,
            dst_ref=target,
            send_sem=send_sem.at[number],
            recv_sem=recv_sem.at[number],
            device_id=(dp, ctx),
            device_id_type=MESH,
        )

    me_x = me_ctx // 4
    me_y = lax.rem(me_ctx, 4)
    me_w = lax.rem(me_z, 4)

    def peers(step):
        return lax.rem(me_x + step, 4), lax.rem(me_y + step, 4)

    def stage_two(mid_x, mid_y, end_x, end_y, number):
        end_x[me_y] = mid_x[me_y]
        end_y[me_x] = mid_y[me_x]
        for step in (2, 1, 3):
            x, y = peers(step)
            remote(mid_x.at[y], end_x.at[me_y], number, me_dp, 4 * me_x + y).start()
            remote(mid_y.at[x], end_y.at[me_x], number + 1, me_dp, 4 * x + me_y).start()

    def four(got):
        return (got[0].astype(F32) + got[1].astype(F32)) + (
            got[2].astype(F32) + got[3].astype(F32)
        )

    def fold(got, mid):
        mid[...] = four(got).astype(BF16).reshape(4, 32, got.shape[2])

    def many(source, target, number, count, dp, ctx):
        return remote(source.at[pl.ds(0, count)], target.at[pl.ds(0, count)], number, dp, ctx)

    loads = [
        pltpu.make_async_copy(source, target, load_sem.at[number])
        for number, (source, target) in enumerate(
            (
                (so_hbm, so_ref),
                (og_hbm, og_ref),
                (x_hbm, x_ref),
                (w_hbm, w_ref),
                (attn_hbm, attn_ref),
                (gain_hbm, gain_ref),
                (rab_hbm, rab_ref),
                (bm_hbm, bm_ref),
                (ro_hbm, ro_ref),
                (wo_hbm, wo_ref),
            )
        )
    ]
    for load in loads:
        load.start()
    low = iota((ROWS, 128), 1) < 64

    loads[0].wait()
    loads[1].wait()
    order = so_ref[...].astype(F32)
    lane = iota((SLOTS, 128), 1)
    place = iota((SLOTS, 128), 0)
    wanted = jnp.sum(jnp.where(lane == slot_of(place), order, 0.0), axis=1, keepdims=True)
    hot = jnp.where(lane.astype(F32) == wanted, 1.0, 0.0).astype(BF16)
    sorted_rows[...] = by_piece(mm(hot, og_ref[...])).astype(BF16).reshape(N_DP, 16, 128)
    arrived[me_dp] = sorted_rows[me_dp]
    loads[2].wait()
    everyone_in()

    def row_copy(step):
        peer = far_dp(me_dp, step)
        return remote(sorted_rows.at[peer], arrived.at[me_dp], 0, peer, me_ctx)

    spread(N_DP, row_copy)
    x_copy = remote(x_ref, other_x, 1, partner, me_ctx)
    x_copy.start()

    x = x_ref[...]
    loads[3].wait()
    pre_v = mm(x, w_ref[:, D : 2 * D])
    sig_v = sigmoid(pre_v)
    slope_ref[:, :D] = sig_v * (1.0 + pre_v * (1.0 - sig_v))
    value = pre_v * sig_v
    pre_k = mm(x, w_ref[:, 3 * D :])
    sig_k = sigmoid(pre_k)
    slope_ref[:, 2 * D :] = sig_k * (1.0 + pre_k * (1.0 - sig_k))
    key = pre_k * sig_k
    for pair in range(H // 2):
        k_two = key[:, pair * 128 : pair * 128 + 128]
        v_two = value[:, pair * 128 : pair * 128 + 128]
        kv_send[2 * pair] = jnp.where(low, k_two, swap(v_two)).astype(BF16)
        kv_send[2 * pair + 1] = jnp.where(low, swap(k_two), v_two).astype(BF16)
    kv_got[me_ctx] = kv_send[own]

    def kv_copy(step):
        peer = lax.rem(me_ctx + step, N_CTX)
        return remote(kv_send.at[peer // 2], kv_got.at[me_ctx], 2, me_dp, peer)

    spread(N_CTX, kv_copy)

    pre_u = mm(x, w_ref[:, :D])
    sig_u = sigmoid(pre_u)
    gating = (pre_u * sig_u).astype(BF16).astype(F32)
    slope_u = sig_u * (1.0 + pre_u * (1.0 - sig_u))
    pre_q = mm(x, w_ref[:, 2 * D : 3 * D])
    sig_q = sigmoid(pre_q)
    slope_ref[:, D : 2 * D] = sig_q * (1.0 + pre_q * (1.0 - sig_q))
    query = (pre_q * sig_q).astype(BF16).astype(F32) * 0.0625
    top = iota((64, 128), 1) < 64

    def stacked(wide, target):
        for pair in range(H // 2):
            upper = wide[:64, pair * 128 : pair * 128 + 128]
            lower = wide[64:, pair * 128 : pair * 128 + 128]
            target[2 * pair] = jnp.where(top, upper, swap(lower)).astype(BF16)
            target[2 * pair + 1] = jnp.where(top, swap(upper), lower).astype(BF16)

    stacked(query, q_send)
    q_got[own] = q_send[own]

    def q_copy(step):
        head = lax.rem(own + step, HALF)
        return remote(q_send.at[head], q_got.at[own], 9, me_dp, member(head, half))

    spread(HALF, q_copy)
    for load in loads[4:]:
        load.wait()
    gain = gain_ref[...]
    attn = attn_ref[...].astype(F32)
    centred = attn - jnp.mean(attn, axis=1, keepdims=True)
    inv_std = lax.rsqrt(jnp.mean(centred * centred, axis=1, keepdims=True) + EPS)
    normal_hat = centred * inv_std
    normed = normal_hat * gain
    mixed_send[...] = (normed * gating).astype(BF16)
    mixed_copy = remote(mixed_send, other_mixed, 3, partner, me_ctx)
    mixed_copy.start()
    gate_scale = normed * slope_u
    hat_scale = gating * gain

    buckets = iota((128, 128), 0)
    own_head = iota((H, 128), 0) == own
    lines = []
    for block in range(REACH):
        chosen = jnp.where(buckets == bm_ref[block : block + 1, :], 1.0, 0.0)
        table = lax.dot_general(
            rab_ref[...],
            chosen,
            (((1,), (0,)), ((), ())),
            precision=lax.Precision.HIGHEST,
            preferred_element_type=F32,
        )
        lines.append(jnp.sum(jnp.where(own_head, table, 0.0), axis=0, keepdims=True) * 0.5)
    blank = jnp.zeros((1, 128), F32)
    for far in range(REACH + 1):
        current = lines[far] if far < REACH else blank
        before = lines[far - 1] if far > 0 else blank
        both = jnp.broadcast_to(jnp.concatenate([current, before], axis=1), (128, 256))
        tile = pltpu.roll(both, 0, 1, stride=1, stride_axis=0)[:, :128]
        bias[(REACH + 1 - far) * 128 : (REACH + 2 - far) * 128, :] = tile
    bias[:128, :] = jnp.zeros((128, 128), F32)
    bias[(REACH + 2) * 128 :, :] = jnp.zeros((128, 128), F32)
    dqt_total[...] = jnp.zeros(dqt_total.shape, F32)
    dkv_total[...] = jnp.zeros(dkv_total.shape, F32)

    taken = ro_ref[...].astype(F32)
    square = iota((128, 128), 0) == iota((128, 128), 1)
    slot_col = jnp.sum(jnp.where(square, taken, 0.0), axis=1, keepdims=True)
    place = iota((ROWS, SLOTS), 1)
    hot = jnp.where(slot_of(place).astype(F32) == slot_col, 1.0, 0.0)
    column = iota((D, 256), 1)
    source_row = iota((D, 256), 0)
    spread_col = (column >> 4) * 32 + (column & 15)
    pick_own = jnp.where(source_row == spread_col + 16 * core, 1.0, 0.0).astype(BF16)
    pick_else = jnp.where(source_row == spread_col + 16 * (1 - core), 1.0, 0.0).astype(BF16)
    zero_core = jnp.broadcast_to(core, (ROWS, 128)) == 0

    def by_core(first, second):
        even = jnp.where(low, first, swap(second))
        odd = jnp.where(low, swap(first), second)
        return (
            jnp.where(zero_core, even, odd).astype(BF16),
            jnp.where(zero_core, odd, even).astype(BF16),
        )

    x_turned[:, :ROWS] = x.astype(F32).T.astype(BF16)
    x_copy.wait_recv()
    x_turned[:, ROWS:] = other_x[...].astype(F32).T.astype(BF16)
    mixed_copy.wait_recv()
    mixed_turned[:, :ROWS] = mixed_send[...].astype(F32).T.astype(BF16)
    mixed_turned[:, ROWS:] = other_mixed[...].astype(F32).T.astype(BF16)
    row_wait = many(sorted_rows, arrived, 0, N_DP - 1, next_dp, me_ctx)
    row_wait.wait_recv()
    owned = pick_pieces(hot, arrived[...].reshape(SLOTS, 128)).astype(BF16)
    grad_z = mm(owned, wo_ref[...], ((1,), (1,)))
    grad_hat = grad_z * hat_scale
    grad_attn = (
        grad_hat
        - jnp.mean(grad_hat, axis=1, keepdims=True)
        - normal_hat * jnp.mean(grad_hat * normal_hat, axis=1, keepdims=True)
    ) * inv_std
    stacked(grad_attn, g_send)
    g_got[own] = g_send[own]

    def g_copy(step):
        head = lax.rem(own + step, HALF)
        return remote(g_send.at[head], g_got.at[own], 4, me_dp, member(head, half))

    spread(HALF, g_copy)

    gate = grad_z * gate_scale
    gate_own = []
    for block in range(2):
        first = gate[:, 256 * block : 256 * block + 128]
        second = gate[:, 256 * block + 128 : 256 * block + 256]
        kept, given = by_core(first, second)
        gate_own.append(kept)
        early_send[:, 128 * block : 128 * block + 128] = given
    early_send[:, 256:] = mm(owned, pick_else).astype(BF16)
    early_copy = remote(early_send, other_early, 5, partner, me_ctx)
    early_copy.start()
    gate_own = jnp.concatenate(gate_own, axis=1)
    owned_own = mm(owned, pick_own).astype(BF16)
    gate = gate.astype(BF16)

    kv_wait = many(kv_got, kv_got, 2, N_CTX - 1, me_dp, next_ctx)
    kv_wait.wait_recv()
    for tile in range(TILES):
        flipped = kv_got[tile].astype(F32).T
        turned[:, tile * 128 : tile * 128 + 128] = flipped[:64].astype(BF16)
    early_copy.wait_recv()
    gate_both = jnp.concatenate([gate_own, other_early[:, :256]], axis=0)
    owned_both = jnp.concatenate([owned_own, other_early[:, 256:]], axis=0)
    first = mm(x_turned[...], gate_both)
    second = mm(mixed_turned[...], owned_both)
    left = iota((D, 128), 1) < 64
    for pair in range(2):
        gate_two = first[:, 128 * pair : 128 * pair + 128]
        out_two = second[:, 128 * pair : 128 * pair + 128]
        early_terms[2 * pair] = jnp.where(left, gate_two, swap(out_two)).astype(BF16)
        early_terms[2 * pair + 1] = jnp.where(left, swap(gate_two), out_two).astype(BF16)
    early_got[me_w] = early_terms[me_w]
    for step in (2, 1, 3):
        peer = lax.rem(me_w + step, 4)
        remote(
            early_terms.at[peer],
            early_got.at[me_w],
            6,
            2 * (me_z - me_w + peer) + core,
            me_ctx,
        ).start()

    q_wait = many(q_send, q_got, 9, HALF - 1, me_dp, next_ctx)
    g_wait = many(g_send, g_got, 4, HALF - 1, me_dp, next_ctx)
    q_wait.wait_recv()
    for index in range(HALF):
        block = q_got[index].astype(F32)
        pairs[index, :64] = jnp.where(top, block, 0.0).astype(BF16)
        pairs[index, 64:128] = jnp.where(top, swap(block), 0.0).astype(BF16)
    g_wait.wait_recv()
    for index in range(HALF):
        block = g_got[index].astype(F32)
        pairs[index, 128:192] = jnp.where(top, 0.0, swap(block)).astype(BF16)
        pairs[index, 192:] = jnp.where(top, 0.0, block).astype(BF16)
    edge_one = len_ref[0, 0]
    edge_two = edge_one + len_ref[0, 1]
    edge_three = edge_two + len_ref[0, 2]

    def meet(pair_index, index):
        keys = kv_got[pl.ds(2 * pair_index, 2)].reshape(256, 128)
        keys_turned = turned[:, pl.ds(pl.multiple_of(pair_index * 256, 256), 256)]
        tile = member(index, half)
        place = tile * 128 + iota((1, 128), 1)
        first = jnp.where(place >= edge_one, edge_one, 0)
        first = jnp.where(place >= edge_two, edge_two, first)
        first = jnp.where(place >= edge_three, edge_three, first)
        both = mm(keys, pairs[index], ((1,), (1,)))
        row = pl.multiple_of((REACH + 1 - tile + 2 * pair_index) * 128, 128)
        scores = both[:, :128] + bias[pl.ds(row, 256), :]
        bent = jnp.tanh(scores)
        key_place = pair_index * 256 + iota((256, 128), 0)
        allowed = (key_place >= first) & (key_place <= place)
        rise = jnp.where(allowed, 1.0 + bent, 0.0)
        weights = scores * rise
        slopes = (both[:, 128:] * (rise + weights * (1.0 - bent))).astype(BF16)
        dqt_total[index] += mm(keys_turned, slopes)
        found = jnp.concatenate([slopes, weights.astype(BF16)], axis=1)
        dkv_total[pair_index] += mm(found, pairs[index])

    def ship(pair_index):
        done = dkv_total[pair_index] * (1.0 / 1024.0)
        dkv_send[pl.ds(2 * pair_index, 2)] = done.astype(BF16).reshape(2, 128, 128)
        for side in range(2):
            peer = 2 * pair_index + side

            @pl.when(peer != me_ctx)
            def _():
                remote(dkv_send.at[peer], dkv_got.at[me_ctx], 14, me_dp, peer).start()

    def one_round(step, carry):
        turn = lax.rem(own + 1 + step, 6)
        for lag in range(3):
            meet(turn, turn + lag)
        meet(jnp.where(turn < 5, turn, 6), jnp.where(turn < 5, turn + 3, 6))
        meet(jnp.where(turn < 4, turn, 11 - turn), jnp.where(turn < 4, turn + 4, 7))
        ship(turn)

        @pl.when(turn >= 4)
        def _():
            ship(11 - turn)

        return carry

    lax.fori_loop(0, 6, one_round, 0)
    dkv_got[me_ctx] = dkv_send[me_ctx]
    dqt_send[...] = (dqt_total[...] * (1.0 / 16384.0)).astype(BF16)
    dqt_got[own] = dqt_send[own]

    def dqt_copy(step):
        index = lax.rem(own + step, HALF)
        return remote(dqt_send.at[index], dqt_got.at[own], 15, me_dp, member(index, half))

    spread(HALF, dqt_copy)

    slot = slot_of(iota((SLOTS, ROWS), 0))
    back_hot = jnp.where(slot == ro_ref[...], 1.0, 0.0).astype(BF16)
    sent = jnp.where(iota((ROWS, 128), 0) == so_ref[...], 1.0, 0.0).astype(BF16)
    place = iota((ROWS, SLOTS), 1)
    spot = jnp.where(iota((ROWS, SLOTS), 0) == slot_of(place), 1.0, 0.0).astype(BF16)
    final_hot = mm(sent, spot)

    dkv_wait = many(dkv_send, dkv_got, 14, N_CTX - 1, me_dp, next_ctx)
    dqt_wait = many(dqt_send, dqt_got, 15, HALF - 1, me_dp, next_ctx)
    dkv_wait.wait_recv()
    grad_k = []
    grad_v = []
    for pair in range(H // 2):
        even = dkv_got[4 * pair].astype(F32) + dkv_got[4 * pair + 1].astype(F32)
        odd = dkv_got[4 * pair + 2].astype(F32) + dkv_got[4 * pair + 3].astype(F32)
        grad_k.append(jnp.where(low, even, swap(odd)))
        grad_v.append(jnp.where(low, swap(even), odd))
    after_v = jnp.concatenate(grad_v, axis=1) * slope_ref[:, :D]
    after_k = jnp.concatenate(grad_k, axis=1) * slope_ref[:, 2 * D :]
    late_own = []

    def split_late(wide, start):
        for block in range(2):
            kept, given = by_core(
                wide[:, 256 * block : 256 * block + 128],
                wide[:, 256 * block + 128 : 256 * block + 256],
            )
            late_own.append(kept)
            late_send[:, start + 128 * block : start + 128 * block + 128] = given

    split_late(after_v, 0)
    split_late(after_k, 256)
    late_copy = remote(
        late_send.at[:, pl.ds(0, 512)], other_late.at[:, pl.ds(0, 512)], 16, partner, me_ctx
    )
    late_copy.start()
    dqt_wait.wait_recv()
    after_q = dqt_got[...].reshape(D, 128).astype(F32).T * slope_ref[:, D : 2 * D]
    split_late(after_q, 512)
    query_copy = remote(
        late_send.at[:, pl.ds(512, 256)], other_late.at[:, pl.ds(512, 256)], 8, partner, me_ctx
    )
    query_copy.start()
    late_copy.wait_recv()
    late_both = jnp.concatenate(
        [jnp.concatenate(late_own[:4], axis=1), other_late[:, :512]], axis=0
    )
    late = mm(x_turned[...], late_both).astype(BF16)
    late_x[...] = late[:, :384].reshape(4, 128, 384)
    late_gx[me_x] = late_x[me_x]
    for step in (2, 1, 3):
        x, y = peers(step)
        remote(late_x.at[x], late_gx.at[me_x], 10, me_dp, 4 * x + me_y).start()
    query_copy.wait_recv()
    query_both = jnp.concatenate(
        [jnp.concatenate(late_own[4:], axis=1), other_late[:, 512:]], axis=0
    )
    late_q = mm(x_turned[...], query_both).astype(BF16)
    for x in range(4):
        for y in range(4):
            row = (4 * x + y) * 32
            late_y[y, 32 * x : 32 * x + 32, :128] = late[row : row + 32, 384:]
            late_y[y, 32 * x : 32 * x + 32, 128:] = late_q[row : row + 32, :]
    late_gy[me_y] = late_y[me_y]
    for step in (2, 1, 3):
        x, y = peers(step)
        remote(late_y.at[y], late_gy.at[me_y], 11, me_dp, 4 * me_x + y).start()
    after = jnp.concatenate([after_v, after_q, after_k], axis=1)
    grad_pre = jnp.concatenate([gate, after.astype(BF16)], axis=1)
    branch = mm(grad_pre, w_ref[...], ((1,), (1,))).astype(BF16)
    back_rows[...] = by_piece(mm(back_hot, branch)).astype(BF16).reshape(N_DP, 16, 128)
    returned[me_dp] = back_rows[me_dp]

    def back_copy(step):
        peer = far_dp(me_dp, step)
        return remote(back_rows.at[peer], returned.at[me_dp], 17, peer, me_ctx)

    spread(N_DP, back_copy)

    early_wait = many(early_terms, early_got, 6, 3, partner, me_ctx)
    early_wait.wait_recv()
    early_spread[...] = four(early_got).astype(BF16).reshape(N_CTX, 32, 128)
    early_parts[me_ctx] = early_spread[me_ctx]

    def early_part_copy(step):
        peer = lax.rem(me_ctx + step, N_CTX)
        return remote(early_spread.at[peer], early_parts.at[me_ctx], 7, me_dp, peer)

    spread(N_CTX, early_part_copy)

    late_wait = [
        many(late_x, late_gx, 10, 3, me_dp, next_ctx),
        many(late_y, late_gy, 11, 3, me_dp, next_ctx),
    ]
    for copy in late_wait:
        copy.wait_recv()
    fold(late_gx, late_mx)
    fold(late_gy, late_my)
    stage_two(late_mx, late_my, late_ex, late_ey, 12)
    back_wait = many(back_rows, returned, 17, N_DP - 1, next_dp, me_ctx)
    back_wait.wait_recv()
    arrival = pick_pieces(final_hot, returned[...].reshape(SLOTS, 128))
    rows_out[...] = (og_ref[...].astype(F32) + arrival).astype(BF16)
    rows_copy = pltpu.make_async_copy(rows_out, rows_hbm, load_sem.at[0])
    rows_copy.start()

    early_end = many(early_spread, early_parts, 7, N_CTX - 1, me_dp, next_ctx)
    early_end.wait_recv()
    early_sum = early_parts[0].astype(F32)
    for source in range(1, N_CTX):
        early_sum = early_sum + early_parts[source].astype(F32)
    late_end = [
        many(late_mx, late_ex, 12, 3, me_dp, next_ctx),
        many(late_my, late_ey, 13, 3, me_dp, next_ctx),
    ]
    for copy in late_end:
        copy.wait_recv()
    late_sum = jnp.concatenate([four(late_ex), four(late_ey)], axis=1)

    low = iota((32, 128), 1) < 64
    group = jnp.broadcast_to(me_w, (32, 128))
    for index in range(N_Z):
        if index < 4:
            block = jnp.where(group == index, early_sum, 0.0)
        else:
            spot = index - 4 if index < 8 else (index if index < 12 else index - 8)
            block = late_sum[:, (spot // 2) * 128 : (spot // 2) * 128 + 128]
            if spot % 2 == 1:
                block = swap(block)
        extra = early_sum
        if index % 4:
            extra = pltpu.roll(extra, 128 - 16 * (index % 4), 1)
        extra = jnp.where(group == index // 4, extra, 0.0)
        last_send[index] = jnp.where(low, block, extra).astype(BF16)
    last_got[me_z] = last_send[me_z]

    def last_copy(step):
        peer = lax.rem(me_z + far_first(step - 1), N_Z)
        return remote(last_send.at[peer], last_got.at[me_z], 18, 2 * peer + core, me_ctx)

    spread(N_Z, last_copy)
    last_wait = many(last_send, last_got, 18, N_Z - 1, 2 * lax.rem(me_z + 1, N_Z) + core, me_ctx)
    last_wait.wait_recv()
    total = last_got[0].astype(F32)
    for source in range(1, N_Z):
        total = total + last_got[source].astype(F32)
    total = total * (1.0 / 256.0)
    uvqk_out[...] = total[:, :64].astype(BF16)
    output_out[...] = total.T[64:80].astype(BF16)
    uvqk_copy = pltpu.make_async_copy(uvqk_out, uvqk_hbm, load_sem.at[1])
    output_copy = pltpu.make_async_copy(output_out, output_hbm, load_sem.at[2])
    uvqk_copy.start()
    output_copy.start()
    for copy in (
        row_wait,
        x_copy,
        kv_wait,
        mixed_copy,
        q_wait,
        g_wait,
        early_copy,
        dkv_wait,
        dqt_wait,
        late_copy,
        query_copy,
        early_wait,
        early_end,
        back_wait,
        last_wait,
        *late_wait,
        *late_end,
    ):
        copy.wait_send()
    rows_copy.wait()
    uvqk_copy.wait()
    output_copy.wait()


def finish_kernel(rows, uvqk, output, rows_out, uvqk_out, output_out, *scratch):
    held, sems = scratch[:3], scratch[3]
    taken = [
        pltpu.make_async_copy(source, target, sems.at[number])
        for number, (source, target) in enumerate(zip((rows, uvqk, output), held))
    ]
    given = [
        pltpu.make_async_copy(source, target, sems.at[3 + number])
        for number, (source, target) in enumerate(zip(held, (rows_out, uvqk_out, output_out)))
    ]
    for copy in taken:
        copy.start()
    for first, second in zip(taken, given):
        first.wait()
        second.start()
    for copy in given:
        copy.wait()


def bf16(*shape):
    return jax.ShapeDtypeStruct(shape, BF16)


def local(
    inputs,
    attn_out,
    out_grad,
    w_uvqk,
    w_output,
    norm_gain,
    rab_table,
    bucket_map,
    lengths,
    send_order,
    recv_order,
):
    taken = (
        inputs,
        attn_out,
        out_grad,
        w_uvqk,
        w_output,
        norm_gain.reshape(1, D),
        rab_table,
        bucket_map.reshape(8, 128),
        send_order,
        recv_order,
    )
    anywhere = pl.BlockSpec(memory_space=pl.ANY)
    scratch = [pltpu.VMEM(array.shape, array.dtype) for array in taken]
    for shape, kind in (
        ((N_DP, 16, 128), BF16),
        ((N_DP, 16, 128), BF16),
        ((H, 128, 128), BF16),
        ((N_CTX, 128, 128), BF16),
        *(((HALF, 64, 128), BF16),) * 4,
        (((REACH + 3) * 128, 128), F32),
        ((64, TILES * 128), BF16),
        ((HALF, 256, 128), BF16),
        ((HALF, 64, 128), F32),
        ((PAIRS, 256, 128), F32),
        ((N_CTX, 128, 128), BF16),
        ((N_CTX, 128, 128), BF16),
        ((HALF, 64, 128), BF16),
        ((HALF, 64, 128), BF16),
        ((ROWS, 3 * D), F32),
        ((N_DP, 16, 128), BF16),
        ((N_DP, 16, 128), BF16),
        ((ROWS, D), BF16),
        ((ROWS, EARLY), BF16),
        ((ROWS, LATE), BF16),
        ((ROWS, D), BF16),
        ((ROWS, D), BF16),
        ((ROWS, EARLY), BF16),
        ((ROWS, LATE), BF16),
        ((D, 2 * ROWS), BF16),
        ((D, 2 * ROWS), BF16),
        ((4, D, 128), BF16),
        ((4, D, 128), BF16),
        ((N_CTX, 32, 128), BF16),
        ((N_CTX, 32, 128), BF16),
        *(((4, 128, LATE // 2), BF16),) * 4,
        *(((4, 32, LATE // 2), BF16),) * 4,
        ((N_Z, 32, 128), BF16),
        ((N_Z, 32, 128), BF16),
        ((ROWS, D), BF16),
        ((32, 64), BF16),
        ((16, 32), BF16),
    ):
        scratch.append(pltpu.VMEM(shape, kind))
    scratch += [
        pltpu.SemaphoreType.DMA((10,)),
        pltpu.SemaphoreType.DMA((19,)),
        pltpu.SemaphoreType.DMA((19,)),
    ]
    shapes = (bf16(ROWS, D), bf16(32, 64), bf16(16, 32))
    results = pl.pallas_call(
        layer_kernel,
        out_shape=shapes,
        in_specs=[pl.BlockSpec(memory_space=pltpu.SMEM)]
        + [anywhere] * len(taken),
        out_specs=(anywhere,) * 3,
        scratch_shapes=scratch,
        compiler_params=pltpu.CompilerParams(
            collective_id=0, has_side_effects=True, vmem_limit_bytes=LIMIT
        ),
    )(lengths, *taken)
    rows, uvqk, output = pl.pallas_call(
        finish_kernel,
        out_shape=shapes,
        in_specs=[anywhere] * 3,
        out_specs=(anywhere,) * 3,
        scratch_shapes=[pltpu.VMEM(shape.shape, shape.dtype) for shape in shapes]
        + [pltpu.SemaphoreType.DMA((6,))],
        compiler_params=pltpu.CompilerParams(vmem_limit_bytes=LIMIT),
    )(*results)
    return rows, uvqk, output.T


def solution(mesh):
    in_specs = (
        P(("dp", "ctx"), None),
        P(("dp", "ctx"), None),
        P(("dp", "ctx"), None),
        P(),
        P(),
        P(),
        P(),
        P(),
        P("dp", None),
        P(("dp", "ctx"), None),
        P(("dp", "ctx"), None),
    )
    out_specs = (P(("dp", "ctx"), None), P("ctx", "dp"), P("ctx", "dp"))
    return jax.shard_map(local, mesh=mesh, in_specs=in_specs, out_specs=out_specs, check_vma=False)
```

```python
import jax
import jax.numpy as jnp
from jax import lax
from jax.experimental import pallas as pl
from jax.experimental.pallas import tpu as pltpu
from jax.sharding import PartitionSpec as P

MESH = pl.DeviceIdType.MESH
F32 = jnp.float32
BF16 = jnp.bfloat16

D = 512
H = 8
ROWS = 128
N_DP = 32
N_CTX = 16
N_Z = 16
TILES = 16
REACH = 8
PAIRS = 8
HALF = 8
SLOTS = 512
EARLY = 512
LATE = 768
EPS = 1e-05
LIMIT = 56 * 1024 * 1024


def mm(left, right, dims=((1,), (0,))):
    return lax.dot_general(left, right, (dims, ((), ())), preferred_element_type=F32)


def iota(shape, dim):
    return lax.broadcasted_iota(jnp.int32, shape, dim)


def slot_of(place):
    return (place >> 4) * 4 + (place & 3)


def piece_of(place):
    return (place >> 2) & 3


def sigmoid(array):
    return 1.0 / (1.0 + jnp.exp(-array))


def half_of(ctx):
    return lax.rem((ctx + 1) // 2, 2)


def member(index, half):
    return 2 * index + lax.rem(half + index, 2)


def by_piece(wide):
    piece = piece_of(iota((SLOTS, 128), 0))
    out = wide[:, :128]
    for part in range(1, 4):
        out = jnp.where(piece == part, wide[:, part * 128 : part * 128 + 128], out)
    return out


def pick_pieces(hot, flat):
    piece = piece_of(iota(hot.shape, 1))
    parts = [mm(jnp.where(piece == part, hot, 0.0).astype(BF16), flat) for part in range(4)]
    return jnp.concatenate(parts, axis=1)


def swap(array):
    return pltpu.roll(array, 64, 1)


def far_first(turn):
    return 8 + jnp.where(lax.rem(turn, 2) == 0, turn // 2, -((turn + 1) // 2))


def far_dp(me_dp, step):
    turn = step - 1
    peer_z = lax.rem(me_dp // 2 + far_first(turn // 2), N_Z)
    return 2 * peer_z + lax.rem(me_dp + 1 + turn, 2)


def announce(me_dp, me_ctx):
    barrier = pltpu.get_barrier_semaphore()

    def tell_dp(step, carry):
        peer = far_dp(me_dp, step)
        pl.semaphore_signal(barrier, inc=1, device_id=(peer, me_ctx), device_id_type=MESH)
        return carry

    def tell_ctx(step, carry):
        peer = lax.rem(me_ctx + step, N_CTX)
        pl.semaphore_signal(barrier, inc=1, device_id=(me_dp, peer), device_id_type=MESH)
        return carry

    lax.fori_loop(1, N_DP, tell_dp, 0)
    lax.fori_loop(1, N_CTX, tell_ctx, 0)


def everyone_in():
    pl.semaphore_wait(pltpu.get_barrier_semaphore(), N_DP - 1 + N_CTX - 1)


def spread(count, copy_to):
    def one(step, carry):
        copy_to(step).start()
        return carry

    lax.fori_loop(1, count, one, 0)


def layer_kernel(
    len_ref,
    x_hbm,
    attn_hbm,
    og_hbm,
    w_hbm,
    wo_hbm,
    gain_hbm,
    rab_hbm,
    bm_hbm,
    so_hbm,
    ro_hbm,
    rows_hbm,
    uvqk_hbm,
    output_hbm,
    x_ref,
    attn_ref,
    og_ref,
    w_ref,
    wo_ref,
    gain_ref,
    rab_ref,
    bm_ref,
    so_ref,
    ro_ref,
    sorted_rows,
    arrived,
    kv_send,
    kv_got,
    q_send,
    q_got,
    g_send,
    g_got,
    bias,
    turned,
    pairs,
    dqt_total,
    dkv_total,
    dkv_send,
    dkv_got,
    dqt_send,
    dqt_got,
    slope_ref,
    back_rows,
    returned,
    mixed_send,
    early_send,
    late_send,
    other_x,
    other_mixed,
    other_early,
    other_late,
    x_turned,
    mixed_turned,
    early_terms,
    early_got,
    early_spread,
    early_parts,
    late_x,
    late_y,
    late_gx,
    late_gy,
    late_mx,
    late_my,
    late_ex,
    late_ey,
    last_send,
    last_got,
    rows_out,
    uvqk_out,
    output_out,
    load_sem,
    send_sem,
    recv_sem,
):
    me_dp = lax.axis_index("dp")
    me_ctx = lax.axis_index("ctx")
    core = lax.rem(me_dp, 2)
    me_z = me_dp // 2
    half = half_of(me_ctx)
    own = me_ctx // 2
    partner = me_dp + 1 - 2 * core
    next_ctx = lax.rem(me_ctx + 1, N_CTX)
    next_dp = lax.rem(me_dp + 1, N_DP)

    announce(me_dp, me_ctx)

    def remote(source, target, number, dp, ctx):
        return pltpu.make_async_remote_copy(
            src_ref=source,
            dst_ref=target,
            send_sem=send_sem.at[number],
            recv_sem=recv_sem.at[number],
            device_id=(dp, ctx),
            device_id_type=MESH,
        )

    me_x = me_ctx // 4
    me_y = lax.rem(me_ctx, 4)
    me_w = lax.rem(me_z, 4)

    def peers(step):
        return lax.rem(me_x + step, 4), lax.rem(me_y + step, 4)

    def stage_two(mid_x, mid_y, end_x, end_y, number):
        end_x[me_y] = mid_x[me_y]
        end_y[me_x] = mid_y[me_x]
        for step in (2, 1, 3):
            x, y = peers(step)
            remote(mid_x.at[y], end_x.at[me_y], number, me_dp, 4 * me_x + y).start()
            remote(mid_y.at[x], end_y.at[me_x], number + 1, me_dp, 4 * x + me_y).start()

    def four(got):
        return (got[0].astype(F32) + got[1].astype(F32)) + (
            got[2].astype(F32) + got[3].astype(F32)
        )

    def fold(got, mid):
        mid[...] = four(got).astype(BF16).reshape(4, 32, got.shape[2])

    def many(source, target, number, count, dp, ctx):
        return remote(source.at[pl.ds(0, count)], target.at[pl.ds(0, count)], number, dp, ctx)

    loads = [
        pltpu.make_async_copy(source, target, load_sem.at[number])
        for number, (source, target) in enumerate(
            (
                (so_hbm, so_ref),
                (og_hbm, og_ref),
                (x_hbm, x_ref),
                (w_hbm, w_ref),
                (attn_hbm, attn_ref),
                (gain_hbm, gain_ref),
                (rab_hbm, rab_ref),
                (bm_hbm, bm_ref),
                (ro_hbm, ro_ref),
                (wo_hbm, wo_ref),
            )
        )
    ]
    for load in loads:
        load.start()
    low = iota((ROWS, 128), 1) < 64

    loads[0].wait()
    loads[1].wait()
    order = so_ref[...].astype(F32)
    lane = iota((SLOTS, 128), 1)
    place = iota((SLOTS, 128), 0)
    wanted = jnp.sum(jnp.where(lane == slot_of(place), order, 0.0), axis=1, keepdims=True)
    hot = jnp.where(lane.astype(F32) == wanted, 1.0, 0.0).astype(BF16)
    sorted_rows[...] = by_piece(mm(hot, og_ref[...])).astype(BF16).reshape(N_DP, 16, 128)
    arrived[me_dp] = sorted_rows[me_dp]
    loads[2].wait()
    everyone_in()

    def row_copy(step):
        peer = far_dp(me_dp, step)
        return remote(sorted_rows.at[peer], arrived.at[me_dp], 0, peer, me_ctx)

    spread(N_DP, row_copy)
    x_copy = remote(x_ref, other_x, 1, partner, me_ctx)
    x_copy.start()

    x = x_ref[...]
    loads[3].wait()
    pre_v = mm(x, w_ref[:, D : 2 * D])
    sig_v = sigmoid(pre_v)
    slope_ref[:, :D] = sig_v * (1.0 + pre_v * (1.0 - sig_v))
    value = pre_v * sig_v
    pre_k = mm(x, w_ref[:, 3 * D :])
    sig_k = sigmoid(pre_k)
    slope_ref[:, 2 * D :] = sig_k * (1.0 + pre_k * (1.0 - sig_k))
    key = pre_k * sig_k
    for pair in range(H // 2):
        k_two = key[:, pair * 128 : pair * 128 + 128]
        v_two = value[:, pair * 128 : pair * 128 + 128]
        kv_send[2 * pair] = jnp.where(low, k_two, swap(v_two)).astype(BF16)
        kv_send[2 * pair + 1] = jnp.where(low, swap(k_two), v_two).astype(BF16)
    kv_got[me_ctx] = kv_send[own]

    def kv_copy(step):
        peer = lax.rem(me_ctx + step, N_CTX)
        return remote(kv_send.at[peer // 2], kv_got.at[me_ctx], 2, me_dp, peer)

    spread(N_CTX, kv_copy)

    pre_u = mm(x, w_ref[:, :D])
    sig_u = sigmoid(pre_u)
    gating = (pre_u * sig_u).astype(BF16).astype(F32)
    slope_u = sig_u * (1.0 + pre_u * (1.0 - sig_u))
    pre_q = mm(x, w_ref[:, 2 * D : 3 * D])
    sig_q = sigmoid(pre_q)
    slope_ref[:, D : 2 * D] = sig_q * (1.0 + pre_q * (1.0 - sig_q))
    query = (pre_q * sig_q).astype(BF16).astype(F32) * 0.0625
    top = iota((64, 128), 1) < 64

    def stacked(wide, target):
        for pair in range(H // 2):
            upper = wide[:64, pair * 128 : pair * 128 + 128]
            lower = wide[64:, pair * 128 : pair * 128 + 128]
            target[2 * pair] = jnp.where(top, upper, swap(lower)).astype(BF16)
            target[2 * pair + 1] = jnp.where(top, swap(upper), lower).astype(BF16)

    stacked(query, q_send)
    q_got[own] = q_send[own]

    def q_copy(step):
        head = lax.rem(own + step, HALF)
        return remote(q_send.at[head], q_got.at[own], 9, me_dp, member(head, half))

    spread(HALF, q_copy)
    for load in loads[4:]:
        load.wait()
    gain = gain_ref[...]
    attn = attn_ref[...].astype(F32)
    centred = attn - jnp.mean(attn, axis=1, keepdims=True)
    inv_std = lax.rsqrt(jnp.mean(centred * centred, axis=1, keepdims=True) + EPS)
    normal_hat = centred * inv_std
    normed = normal_hat * gain
    mixed_send[...] = (normed * gating).astype(BF16)
    mixed_copy = remote(mixed_send, other_mixed, 3, partner, me_ctx)
    mixed_copy.start()
    gate_scale = normed * slope_u
    hat_scale = gating * gain

    buckets = iota((128, 128), 0)
    own_head = iota((H, 128), 0) == own
    lines = []
    for block in range(REACH):
        chosen = jnp.where(buckets == bm_ref[block : block + 1, :], 1.0, 0.0)
        table = lax.dot_general(
            rab_ref[...],
            chosen,
            (((1,), (0,)), ((), ())),
            precision=lax.Precision.HIGHEST,
            preferred_element_type=F32,
        )
        lines.append(jnp.sum(jnp.where(own_head, table, 0.0), axis=0, keepdims=True) * 0.5)
    blank = jnp.zeros((1, 128), F32)
    for far in range(REACH + 1):
        current = lines[far] if far < REACH else blank
        before = lines[far - 1] if far > 0 else blank
        both = jnp.broadcast_to(jnp.concatenate([current, before], axis=1), (128, 256))
        tile = pltpu.roll(both, 0, 1, stride=1, stride_axis=0)[:, :128]
        bias[(REACH + 1 - far) * 128 : (REACH + 2 - far) * 128, :] = tile
    bias[:128, :] = jnp.zeros((128, 128), F32)
    bias[(REACH + 2) * 128 :, :] = jnp.zeros((128, 128), F32)
    dqt_total[...] = jnp.zeros(dqt_total.shape, F32)
    dkv_total[...] = jnp.zeros(dkv_total.shape, F32)

    taken = ro_ref[...].astype(F32)
    square = iota((128, 128), 0) == iota((128, 128), 1)
    slot_col = jnp.sum(jnp.where(square, taken, 0.0), axis=1, keepdims=True)
    place = iota((ROWS, SLOTS), 1)
    hot = jnp.where(slot_of(place).astype(F32) == slot_col, 1.0, 0.0)
    column = iota((D, 256), 1)
    source_row = iota((D, 256), 0)
    spread_col = (column >> 4) * 32 + (column & 15)
    pick_own = jnp.where(source_row == spread_col + 16 * core, 1.0, 0.0).astype(BF16)
    pick_else = jnp.where(source_row == spread_col + 16 * (1 - core), 1.0, 0.0).astype(BF16)
    zero_core = jnp.broadcast_to(core, (ROWS, 128)) == 0

    def by_core(first, second):
        even = jnp.where(low, first, swap(second))
        odd = jnp.where(low, swap(first), second)
        return (
            jnp.where(zero_core, even, odd).astype(BF16),
            jnp.where(zero_core, odd, even).astype(BF16),
        )

    x_turned[:, :ROWS] = x.astype(F32).T.astype(BF16)
    x_copy.wait_recv()
    x_turned[:, ROWS:] = other_x[...].astype(F32).T.astype(BF16)
    mixed_copy.wait_recv()
    mixed_turned[:, :ROWS] = mixed_send[...].astype(F32).T.astype(BF16)
    mixed_turned[:, ROWS:] = other_mixed[...].astype(F32).T.astype(BF16)
    row_wait = many(sorted_rows, arrived, 0, N_DP - 1, next_dp, me_ctx)
    row_wait.wait_recv()
    owned = pick_pieces(hot, arrived[...].reshape(SLOTS, 128)).astype(BF16)
    grad_z = mm(owned, wo_ref[...], ((1,), (1,)))
    grad_hat = grad_z * hat_scale
    grad_attn = (
        grad_hat
        - jnp.mean(grad_hat, axis=1, keepdims=True)
        - normal_hat * jnp.mean(grad_hat * normal_hat, axis=1, keepdims=True)
    ) * inv_std
    stacked(grad_attn, g_send)
    g_got[own] = g_send[own]

    def g_copy(step):
        head = lax.rem(own + step, HALF)
        return remote(g_send.at[head], g_got.at[own], 4, me_dp, member(head, half))

    spread(HALF, g_copy)

    gate = grad_z * gate_scale
    gate_own = []
    for block in range(2):
        first = gate[:, 256 * block : 256 * block + 128]
        second = gate[:, 256 * block + 128 : 256 * block + 256]
        kept, given = by_core(first, second)
        gate_own.append(kept)
        early_send[:, 128 * block : 128 * block + 128] = given
    early_send[:, 256:] = mm(owned, pick_else).astype(BF16)
    early_copy = remote(early_send, other_early, 5, partner, me_ctx)
    early_copy.start()
    gate_own = jnp.concatenate(gate_own, axis=1)
    owned_own = mm(owned, pick_own).astype(BF16)
    gate = gate.astype(BF16)

    kv_wait = many(kv_got, kv_got, 2, N_CTX - 1, me_dp, next_ctx)
    kv_wait.wait_recv()
    for tile in range(TILES):
        flipped = kv_got[tile].astype(F32).T
        turned[:, tile * 128 : tile * 128 + 128] = flipped[:64].astype(BF16)
    early_copy.wait_recv()
    gate_both = jnp.concatenate([gate_own, other_early[:, :256]], axis=0)
    owned_both = jnp.concatenate([owned_own, other_early[:, 256:]], axis=0)
    first = mm(x_turned[...], gate_both)
    second = mm(mixed_turned[...], owned_both)
    left = iota((D, 128), 1) < 64
    for pair in range(2):
        gate_two = first[:, 128 * pair : 128 * pair + 128]
        out_two = second[:, 128 * pair : 128 * pair + 128]
        early_terms[2 * pair] = jnp.where(left, gate_two, swap(out_two)).astype(BF16)
        early_terms[2 * pair + 1] = jnp.where(left, swap(gate_two), out_two).astype(BF16)
    early_got[me_w] = early_terms[me_w]
    for step in (2, 1, 3):
        peer = lax.rem(me_w + step, 4)
        remote(
            early_terms.at[peer],
            early_got.at[me_w],
            6,
            2 * (me_z - me_w + peer) + core,
            me_ctx,
        ).start()

    q_wait = many(q_send, q_got, 9, HALF - 1, me_dp, next_ctx)
    g_wait = many(g_send, g_got, 4, HALF - 1, me_dp, next_ctx)
    q_wait.wait_recv()
    for index in range(HALF):
        block = q_got[index].astype(F32)
        pairs[index, :64] = jnp.where(top, block, 0.0).astype(BF16)
        pairs[index, 64:128] = jnp.where(top, swap(block), 0.0).astype(BF16)
    g_wait.wait_recv()
    for index in range(HALF):
        block = g_got[index].astype(F32)
        pairs[index, 128:192] = jnp.where(top, 0.0, swap(block)).astype(BF16)
        pairs[index, 192:] = jnp.where(top, 0.0, block).astype(BF16)
    edge_one = len_ref[0, 0]
    edge_two = edge_one + len_ref[0, 1]
    edge_three = edge_two + len_ref[0, 2]

    def meet(pair_index, index):
        keys = kv_got[pl.ds(2 * pair_index, 2)].reshape(256, 128)
        tile = member(index, half)
        place = tile * 128 + iota((1, 128), 1)
        first = jnp.where(place >= edge_one, edge_one, 0)
        first = jnp.where(place >= edge_two, edge_two, first)
        first = jnp.where(place >= edge_three, edge_three, first)
        both = mm(keys, pairs[index], ((1,), (1,)))
        row = pl.multiple_of((REACH + 1 - tile + 2 * pair_index) * 128, 128)
        scores = both[:, :128] + bias[pl.ds(row, 256), :]
        bent = jnp.tanh(scores)
        key_place = pair_index * 256 + iota((256, 128), 0)
        allowed = (key_place >= first) & (key_place <= place)
        rise = jnp.where(allowed, 1.0 + bent, 0.0)
        weights = scores * rise
        slopes = (both[:, 128:] * (rise + weights * (1.0 - bent))).astype(BF16)
        return jnp.concatenate([slopes, weights.astype(BF16)], axis=1)

    def ship(pair_index):
        done = dkv_total[pair_index] * (1.0 / 1024.0)
        dkv_send[pl.ds(2 * pair_index, 2)] = done.astype(BF16).reshape(2, 128, 128)
        for side in range(2):
            peer = 2 * pair_index + side

            @pl.when(peer != me_ctx)
            def _():
                remote(dkv_send.at[peer], dkv_got.at[me_ctx], 14, me_dp, peer).start()

    def one_round(step, carry):
        turn = lax.rem(own + 1 + step, 6)
        spots = [
            (turn, turn),
            (turn, turn + 1),
            (turn, turn + 2),
            (jnp.where(turn < 5, turn, 6), jnp.where(turn < 5, turn + 3, 6)),
            (jnp.where(turn < 4, turn, 11 - turn), jnp.where(turn < 4, turn + 4, 7)),
        ]
        found = [meet(pair_index, index) for pair_index, index in spots]
        for (pair_index, index), block in zip(spots, found):
            keys_turned = turned[:, pl.ds(pl.multiple_of(pair_index * 256, 256), 256)]
            dqt_total[index] += mm(keys_turned, block[:, :128])
        dkv_total[turn] += mm(
            jnp.concatenate(found[:3], axis=1), pairs[pl.ds(turn, 3)].reshape(768, 128)
        )
        for (pair_index, index), block in zip(spots[3:], found[3:]):
            dkv_total[pair_index] += mm(block, pairs[index])
        ship(turn)

        @pl.when(turn >= 4)
        def _():
            ship(11 - turn)

        return carry

    lax.fori_loop(0, 6, one_round, 0)
    dkv_got[me_ctx] = dkv_send[me_ctx]
    dqt_send[...] = (dqt_total[...] * (1.0 / 16384.0)).astype(BF16)
    dqt_got[own] = dqt_send[own]

    def dqt_copy(step):
        index = lax.rem(own + step, HALF)
        return remote(dqt_send.at[index], dqt_got.at[own], 15, me_dp, member(index, half))

    spread(HALF, dqt_copy)

    slot = slot_of(iota((SLOTS, ROWS), 0))
    back_hot = jnp.where(slot == ro_ref[...], 1.0, 0.0).astype(BF16)
    sent = jnp.where(iota((ROWS, 128), 0) == so_ref[...], 1.0, 0.0).astype(BF16)
    place = iota((ROWS, SLOTS), 1)
    spot = jnp.where(iota((ROWS, SLOTS), 0) == slot_of(place), 1.0, 0.0).astype(BF16)
    final_hot = mm(sent, spot)

    dkv_wait = many(dkv_send, dkv_got, 14, N_CTX - 1, me_dp, next_ctx)
    dqt_wait = many(dqt_send, dqt_got, 15, HALF - 1, me_dp, next_ctx)
    dkv_wait.wait_recv()
    grad_k = []
    grad_v = []
    for pair in range(H // 2):
        even = dkv_got[4 * pair].astype(F32) + dkv_got[4 * pair + 1].astype(F32)
        odd = dkv_got[4 * pair + 2].astype(F32) + dkv_got[4 * pair + 3].astype(F32)
        grad_k.append(jnp.where(low, even, swap(odd)))
        grad_v.append(jnp.where(low, swap(even), odd))
    after_v = jnp.concatenate(grad_v, axis=1) * slope_ref[:, :D]
    after_k = jnp.concatenate(grad_k, axis=1) * slope_ref[:, 2 * D :]
    late_own = []

    def split_late(wide, start):
        for block in range(2):
            kept, given = by_core(
                wide[:, 256 * block : 256 * block + 128],
                wide[:, 256 * block + 128 : 256 * block + 256],
            )
            late_own.append(kept)
            late_send[:, start + 128 * block : start + 128 * block + 128] = given

    split_late(after_v, 0)
    split_late(after_k, 256)
    late_copy = remote(
        late_send.at[:, pl.ds(0, 512)], other_late.at[:, pl.ds(0, 512)], 16, partner, me_ctx
    )
    late_copy.start()
    dqt_wait.wait_recv()
    after_q = dqt_got[...].reshape(D, 128).astype(F32).T * slope_ref[:, D : 2 * D]
    split_late(after_q, 512)
    query_copy = remote(
        late_send.at[:, pl.ds(512, 256)], other_late.at[:, pl.ds(512, 256)], 8, partner, me_ctx
    )
    query_copy.start()
    late_copy.wait_recv()
    late_both = jnp.concatenate(
        [jnp.concatenate(late_own[:4], axis=1), other_late[:, :512]], axis=0
    )
    late = mm(x_turned[...], late_both).astype(BF16)
    late_x[...] = late[:, :384].reshape(4, 128, 384)
    late_gx[me_x] = late_x[me_x]
    for step in (2, 1, 3):
        x, y = peers(step)
        remote(late_x.at[x], late_gx.at[me_x], 10, me_dp, 4 * x + me_y).start()
    query_copy.wait_recv()
    query_both = jnp.concatenate(
        [jnp.concatenate(late_own[4:], axis=1), other_late[:, 512:]], axis=0
    )
    late_q = mm(x_turned[...], query_both).astype(BF16)
    for x in range(4):
        for y in range(4):
            row = (4 * x + y) * 32
            late_y[y, 32 * x : 32 * x + 32, :128] = late[row : row + 32, 384:]
            late_y[y, 32 * x : 32 * x + 32, 128:] = late_q[row : row + 32, :]
    late_gy[me_y] = late_y[me_y]
    for step in (2, 1, 3):
        x, y = peers(step)
        remote(late_y.at[y], late_gy.at[me_y], 11, me_dp, 4 * me_x + y).start()
    after = jnp.concatenate([after_v, after_q, after_k], axis=1)
    grad_pre = jnp.concatenate([gate, after.astype(BF16)], axis=1)
    branch = mm(grad_pre, w_ref[...], ((1,), (1,))).astype(BF16)
    back_rows[...] = by_piece(mm(back_hot, branch)).astype(BF16).reshape(N_DP, 16, 128)
    returned[me_dp] = back_rows[me_dp]

    def back_copy(step):
        peer = far_dp(me_dp, step)
        return remote(back_rows.at[peer], returned.at[me_dp], 17, peer, me_ctx)

    spread(N_DP, back_copy)

    early_wait = many(early_terms, early_got, 6, 3, partner, me_ctx)
    early_wait.wait_recv()
    early_spread[...] = four(early_got).astype(BF16).reshape(N_CTX, 32, 128)
    early_parts[me_ctx] = early_spread[me_ctx]

    def early_part_copy(step):
        peer = lax.rem(me_ctx + step, N_CTX)
        return remote(early_spread.at[peer], early_parts.at[me_ctx], 7, me_dp, peer)

    spread(N_CTX, early_part_copy)

    late_wait = [
        many(late_x, late_gx, 10, 3, me_dp, next_ctx),
        many(late_y, late_gy, 11, 3, me_dp, next_ctx),
    ]
    for copy in late_wait:
        copy.wait_recv()
    fold(late_gx, late_mx)
    fold(late_gy, late_my)
    stage_two(late_mx, late_my, late_ex, late_ey, 12)
    back_wait = many(back_rows, returned, 17, N_DP - 1, next_dp, me_ctx)
    back_wait.wait_recv()
    arrival = pick_pieces(final_hot, returned[...].reshape(SLOTS, 128))
    rows_out[...] = (og_ref[...].astype(F32) + arrival).astype(BF16)
    rows_copy = pltpu.make_async_copy(rows_out, rows_hbm, load_sem.at[0])
    rows_copy.start()

    early_end = many(early_spread, early_parts, 7, N_CTX - 1, me_dp, next_ctx)
    early_end.wait_recv()
    early_sum = early_parts[0].astype(F32)
    for source in range(1, N_CTX):
        early_sum = early_sum + early_parts[source].astype(F32)
    late_end = [
        many(late_mx, late_ex, 12, 3, me_dp, next_ctx),
        many(late_my, late_ey, 13, 3, me_dp, next_ctx),
    ]
    for copy in late_end:
        copy.wait_recv()
    late_sum = jnp.concatenate([four(late_ex), four(late_ey)], axis=1)

    low = iota((32, 128), 1) < 64
    group = jnp.broadcast_to(me_w, (32, 128))
    for index in range(N_Z):
        if index < 4:
            block = jnp.where(group == index, early_sum, 0.0)
        else:
            spot = index - 4 if index < 8 else (index if index < 12 else index - 8)
            block = late_sum[:, (spot // 2) * 128 : (spot // 2) * 128 + 128]
            if spot % 2 == 1:
                block = swap(block)
        extra = early_sum
        if index % 4:
            extra = pltpu.roll(extra, 128 - 16 * (index % 4), 1)
        extra = jnp.where(group == index // 4, extra, 0.0)
        last_send[index] = jnp.where(low, block, extra).astype(BF16)
    last_got[me_z] = last_send[me_z]

    def last_copy(step):
        peer = lax.rem(me_z + far_first(step - 1), N_Z)
        return remote(last_send.at[peer], last_got.at[me_z], 18, 2 * peer + core, me_ctx)

    spread(N_Z, last_copy)
    last_wait = many(last_send, last_got, 18, N_Z - 1, 2 * lax.rem(me_z + 1, N_Z) + core, me_ctx)
    last_wait.wait_recv()
    total = last_got[0].astype(F32)
    for source in range(1, N_Z):
        total = total + last_got[source].astype(F32)
    total = total * (1.0 / 256.0)
    uvqk_out[...] = total[:, :64].astype(BF16)
    output_out[...] = total.T[64:80].astype(BF16)
    uvqk_copy = pltpu.make_async_copy(uvqk_out, uvqk_hbm, load_sem.at[1])
    output_copy = pltpu.make_async_copy(output_out, output_hbm, load_sem.at[2])
    uvqk_copy.start()
    output_copy.start()
    for copy in (
        row_wait,
        x_copy,
        kv_wait,
        mixed_copy,
        q_wait,
        g_wait,
        early_copy,
        dkv_wait,
        dqt_wait,
        late_copy,
        query_copy,
        early_wait,
        early_end,
        back_wait,
        last_wait,
        *late_wait,
        *late_end,
    ):
        copy.wait_send()
    rows_copy.wait()
    uvqk_copy.wait()
    output_copy.wait()


def finish_kernel(rows, uvqk, output, rows_out, uvqk_out, output_out, *scratch):
    held, sems = scratch[:3], scratch[3]
    taken = [
        pltpu.make_async_copy(source, target, sems.at[number])
        for number, (source, target) in enumerate(zip((rows, uvqk, output), held))
    ]
    given = [
        pltpu.make_async_copy(source, target, sems.at[3 + number])
        for number, (source, target) in enumerate(zip(held, (rows_out, uvqk_out, output_out)))
    ]
    for copy in taken:
        copy.start()
    for first, second in zip(taken, given):
        first.wait()
        second.start()
    for copy in given:
        copy.wait()


def bf16(*shape):
    return jax.ShapeDtypeStruct(shape, BF16)


def local(
    inputs,
    attn_out,
    out_grad,
    w_uvqk,
    w_output,
    norm_gain,
    rab_table,
    bucket_map,
    lengths,
    send_order,
    recv_order,
):
    taken = (
        inputs,
        attn_out,
        out_grad,
        w_uvqk,
        w_output,
        norm_gain.reshape(1, D),
        rab_table,
        bucket_map.reshape(8, 128),
        send_order,
        recv_order,
    )
    anywhere = pl.BlockSpec(memory_space=pl.ANY)
    scratch = [pltpu.VMEM(array.shape, array.dtype) for array in taken]
    for shape, kind in (
        ((N_DP, 16, 128), BF16),
        ((N_DP, 16, 128), BF16),
        ((H, 128, 128), BF16),
        ((N_CTX, 128, 128), BF16),
        *(((HALF, 64, 128), BF16),) * 4,
        (((REACH + 3) * 128, 128), F32),
        ((64, TILES * 128), BF16),
        ((HALF, 256, 128), BF16),
        ((HALF, 64, 128), F32),
        ((PAIRS, 256, 128), F32),
        ((N_CTX, 128, 128), BF16),
        ((N_CTX, 128, 128), BF16),
        ((HALF, 64, 128), BF16),
        ((HALF, 64, 128), BF16),
        ((ROWS, 3 * D), F32),
        ((N_DP, 16, 128), BF16),
        ((N_DP, 16, 128), BF16),
        ((ROWS, D), BF16),
        ((ROWS, EARLY), BF16),
        ((ROWS, LATE), BF16),
        ((ROWS, D), BF16),
        ((ROWS, D), BF16),
        ((ROWS, EARLY), BF16),
        ((ROWS, LATE), BF16),
        ((D, 2 * ROWS), BF16),
        ((D, 2 * ROWS), BF16),
        ((4, D, 128), BF16),
        ((4, D, 128), BF16),
        ((N_CTX, 32, 128), BF16),
        ((N_CTX, 32, 128), BF16),
        *(((4, 128, LATE // 2), BF16),) * 4,
        *(((4, 32, LATE // 2), BF16),) * 4,
        ((N_Z, 32, 128), BF16),
        ((N_Z, 32, 128), BF16),
        ((ROWS, D), BF16),
        ((32, 64), BF16),
        ((16, 32), BF16),
    ):
        scratch.append(pltpu.VMEM(shape, kind))
    scratch += [
        pltpu.SemaphoreType.DMA((10,)),
        pltpu.SemaphoreType.DMA((19,)),
        pltpu.SemaphoreType.DMA((19,)),
    ]
    shapes = (bf16(ROWS, D), bf16(32, 64), bf16(16, 32))
    results = pl.pallas_call(
        layer_kernel,
        out_shape=shapes,
        in_specs=[pl.BlockSpec(memory_space=pltpu.SMEM)]
        + [anywhere] * len(taken),
        out_specs=(anywhere,) * 3,
        scratch_shapes=scratch,
        compiler_params=pltpu.CompilerParams(
            collective_id=0, has_side_effects=True, vmem_limit_bytes=LIMIT
        ),
    )(lengths, *taken)
    rows, uvqk, output = pl.pallas_call(
        finish_kernel,
        out_shape=shapes,
        in_specs=[anywhere] * 3,
        out_specs=(anywhere,) * 3,
        scratch_shapes=[pltpu.VMEM(shape.shape, shape.dtype) for shape in shapes]
        + [pltpu.SemaphoreType.DMA((6,))],
        compiler_params=pltpu.CompilerParams(vmem_limit_bytes=LIMIT),
    )(*results)
    return rows, uvqk, output.T


def solution(mesh):
    in_specs = (
        P(("dp", "ctx"), None),
        P(("dp", "ctx"), None),
        P(("dp", "ctx"), None),
        P(),
        P(),
        P(),
        P(),
        P(),
        P("dp", None),
        P(("dp", "ctx"), None),
        P(("dp", "ctx"), None),
    )
    out_specs = (P(("dp", "ctx"), None), P("ctx", "dp"), P("ctx", "dp"))
    return jax.shard_map(local, mesh=mesh, in_specs=in_specs, out_specs=out_specs, check_vma=False)
```

```python
import jax
import jax.numpy as jnp
from jax import lax
from jax.experimental import pallas as pl
from jax.experimental.pallas import tpu as pltpu
from jax.sharding import PartitionSpec as P

MESH = pl.DeviceIdType.MESH
F32 = jnp.float32
BF16 = jnp.bfloat16

D = 512
H = 8
ROWS = 128
N_DP = 32
N_CTX = 16
N_Z = 16
TILES = 16
REACH = 8
PAIRS = 8
HALF = 8
SLOTS = 512
EARLY = 512
LATE = 768
EPS = 1e-05
LIMIT = 56 * 1024 * 1024


def mm(left, right, dims=((1,), (0,))):
    return lax.dot_general(left, right, (dims, ((), ())), preferred_element_type=F32)


def iota(shape, dim):
    return lax.broadcasted_iota(jnp.int32, shape, dim)


def slot_of(place):
    return (place >> 4) * 4 + (place & 3)


def piece_of(place):
    return (place >> 2) & 3


def sigmoid(array):
    return 1.0 / (1.0 + jnp.exp(-array))


def half_of(ctx):
    return lax.rem((ctx + 1) // 2, 2)


def member(index, half):
    return 2 * index + lax.rem(half + index, 2)


def by_piece(wide):
    piece = piece_of(iota((SLOTS, 128), 0))
    out = wide[:, :128]
    for part in range(1, 4):
        out = jnp.where(piece == part, wide[:, part * 128 : part * 128 + 128], out)
    return out


def pick_pieces(hot, flat):
    piece = piece_of(iota(hot.shape, 1))
    parts = [mm(jnp.where(piece == part, hot, 0.0).astype(BF16), flat) for part in range(4)]
    return jnp.concatenate(parts, axis=1)


def swap(array):
    return pltpu.roll(array, 64, 1)


def far_first(turn):
    return 8 + jnp.where(lax.rem(turn, 2) == 0, turn // 2, -((turn + 1) // 2))


def far_dp(me_dp, step):
    turn = step - 1
    peer_z = lax.rem(me_dp // 2 + far_first(turn // 2), N_Z)
    return 2 * peer_z + lax.rem(me_dp + 1 + turn, 2)


def announce(me_dp, me_ctx):
    barrier = pltpu.get_barrier_semaphore()

    def tell_dp(step, carry):
        peer = far_dp(me_dp, step)
        pl.semaphore_signal(barrier, inc=1, device_id=(peer, me_ctx), device_id_type=MESH)
        return carry

    def tell_ctx(step, carry):
        peer = lax.rem(me_ctx + step, N_CTX)
        pl.semaphore_signal(barrier, inc=1, device_id=(me_dp, peer), device_id_type=MESH)
        return carry

    lax.fori_loop(1, N_DP, tell_dp, 0)
    lax.fori_loop(1, N_CTX, tell_ctx, 0)


def everyone_in():
    pl.semaphore_wait(pltpu.get_barrier_semaphore(), N_DP - 1 + N_CTX - 1)


def spread(count, copy_to):
    def one(step, carry):
        copy_to(step).start()
        return carry

    lax.fori_loop(1, count, one, 0)


def layer_kernel(
    len_ref,
    x_hbm,
    attn_hbm,
    og_hbm,
    w_hbm,
    wo_hbm,
    gain_hbm,
    rab_hbm,
    bm_hbm,
    so_hbm,
    ro_hbm,
    rows_hbm,
    uvqk_hbm,
    output_hbm,
    x_ref,
    attn_ref,
    og_ref,
    w_ref,
    wo_ref,
    gain_ref,
    rab_ref,
    bm_ref,
    so_ref,
    ro_ref,
    sorted_rows,
    arrived,
    cross_send,
    cross_got,
    gathered,
    kv_send,
    kv_got,
    q_send,
    q_got,
    g_send,
    g_got,
    bias,
    turned,
    pairs,
    dqt_total,
    dkv_total,
    dkv_send,
    dkv_got,
    dqt_send,
    dqt_got,
    slope_ref,
    back_rows,
    returned,
    mixed_send,
    early_send,
    late_send,
    other_x,
    other_mixed,
    other_early,
    other_late,
    x_turned,
    mixed_turned,
    early_terms,
    early_got,
    early_spread,
    early_parts,
    late_x,
    late_y,
    late_gx,
    late_gy,
    late_mx,
    late_my,
    late_ex,
    late_ey,
    last_send,
    last_got,
    rows_out,
    uvqk_out,
    output_out,
    load_sem,
    send_sem,
    recv_sem,
):
    me_dp = lax.axis_index("dp")
    me_ctx = lax.axis_index("ctx")
    core = lax.rem(me_dp, 2)
    me_z = me_dp // 2
    half = half_of(me_ctx)
    own = me_ctx // 2
    partner = me_dp + 1 - 2 * core
    next_ctx = lax.rem(me_ctx + 1, N_CTX)
    next_dp = lax.rem(me_dp + 1, N_DP)

    announce(me_dp, me_ctx)

    def remote(source, target, number, dp, ctx):
        return pltpu.make_async_remote_copy(
            src_ref=source,
            dst_ref=target,
            send_sem=send_sem.at[number],
            recv_sem=recv_sem.at[number],
            device_id=(dp, ctx),
            device_id_type=MESH,
        )

    me_x = me_ctx // 4
    me_y = lax.rem(me_ctx, 4)
    me_w = lax.rem(me_z, 4)

    def peers(step):
        return lax.rem(me_x + step, 4), lax.rem(me_y + step, 4)

    def stage_two(mid_x, mid_y, end_x, end_y, number):
        end_x[me_y] = mid_x[me_y]
        end_y[me_x] = mid_y[me_x]
        for step in (2, 1, 3):
            x, y = peers(step)
            remote(mid_x.at[y], end_x.at[me_y], number, me_dp, 4 * me_x + y).start()
            remote(mid_y.at[x], end_y.at[me_x], number + 1, me_dp, 4 * x + me_y).start()

    def four(got):
        return (got[0].astype(F32) + got[1].astype(F32)) + (
            got[2].astype(F32) + got[3].astype(F32)
        )

    def fold(got, mid):
        mid[...] = four(got).astype(BF16).reshape(4, 32, got.shape[2])

    def many(source, target, number, count, dp, ctx):
        return remote(source.at[pl.ds(0, count)], target.at[pl.ds(0, count)], number, dp, ctx)

    loads = [
        pltpu.make_async_copy(source, target, load_sem.at[number])
        for number, (source, target) in enumerate(
            (
                (so_hbm, so_ref),
                (og_hbm, og_ref),
                (x_hbm, x_ref),
                (w_hbm, w_ref),
                (attn_hbm, attn_ref),
                (gain_hbm, gain_ref),
                (rab_hbm, rab_ref),
                (bm_hbm, bm_ref),
                (ro_hbm, ro_ref),
                (wo_hbm, wo_ref),
            )
        )
    ]
    for load in loads:
        load.start()
    low = iota((ROWS, 128), 1) < 64

    loads[0].wait()
    loads[1].wait()
    order = so_ref[...].astype(F32)
    lane = iota((SLOTS, 128), 1)
    place = iota((SLOTS, 128), 0)
    wanted = jnp.sum(jnp.where(lane == slot_of(place), order, 0.0), axis=1, keepdims=True)
    hot = jnp.where(lane.astype(F32) == wanted, 1.0, 0.0).astype(BF16)
    sorted_rows[...] = by_piece(mm(hot, og_ref[...])).astype(BF16).reshape(N_Z, 2, 16, 128)
    arrived[me_z] = sorted_rows[me_z]
    loads[2].wait()
    everyone_in()

    def row_copy(step):
        peer = lax.rem(me_z + far_first(step - 1), N_Z)
        return remote(sorted_rows.at[peer], arrived.at[me_z], 0, 2 * peer + core, me_ctx)

    spread(N_Z, row_copy)
    x_copy = remote(x_ref, other_x, 1, partner, me_ctx)
    x_copy.start()

    x = x_ref[...]
    loads[3].wait()
    pre_v = mm(x, w_ref[:, D : 2 * D])
    sig_v = sigmoid(pre_v)
    slope_ref[:, :D] = sig_v * (1.0 + pre_v * (1.0 - sig_v))
    value = pre_v * sig_v
    pre_k = mm(x, w_ref[:, 3 * D :])
    sig_k = sigmoid(pre_k)
    slope_ref[:, 2 * D :] = sig_k * (1.0 + pre_k * (1.0 - sig_k))
    key = pre_k * sig_k
    for pair in range(H // 2):
        k_two = key[:, pair * 128 : pair * 128 + 128]
        v_two = value[:, pair * 128 : pair * 128 + 128]
        kv_send[2 * pair] = jnp.where(low, k_two, swap(v_two)).astype(BF16)
        kv_send[2 * pair + 1] = jnp.where(low, swap(k_two), v_two).astype(BF16)
    kv_got[me_ctx] = kv_send[own]

    def kv_copy(step):
        peer = lax.rem(me_ctx + step, N_CTX)
        return remote(kv_send.at[peer // 2], kv_got.at[me_ctx], 2, me_dp, peer)

    spread(N_CTX, kv_copy)

    pre_u = mm(x, w_ref[:, :D])
    sig_u = sigmoid(pre_u)
    gating = (pre_u * sig_u).astype(BF16).astype(F32)
    slope_u = sig_u * (1.0 + pre_u * (1.0 - sig_u))
    pre_q = mm(x, w_ref[:, 2 * D : 3 * D])
    sig_q = sigmoid(pre_q)
    slope_ref[:, D : 2 * D] = sig_q * (1.0 + pre_q * (1.0 - sig_q))
    query = (pre_q * sig_q).astype(BF16).astype(F32) * 0.0625
    top = iota((64, 128), 1) < 64

    def stacked(wide, target):
        for pair in range(H // 2):
            upper = wide[:64, pair * 128 : pair * 128 + 128]
            lower = wide[64:, pair * 128 : pair * 128 + 128]
            target[2 * pair] = jnp.where(top, upper, swap(lower)).astype(BF16)
            target[2 * pair + 1] = jnp.where(top, swap(upper), lower).astype(BF16)

    stacked(query, q_send)
    q_got[own] = q_send[own]

    def q_copy(step):
        head = lax.rem(own + step, HALF)
        return remote(q_send.at[head], q_got.at[own], 9, me_dp, member(head, half))

    spread(HALF, q_copy)
    for load in loads[4:]:
        load.wait()
    gain = gain_ref[...]
    attn = attn_ref[...].astype(F32)
    centred = attn - jnp.mean(attn, axis=1, keepdims=True)
    inv_std = lax.rsqrt(jnp.mean(centred * centred, axis=1, keepdims=True) + EPS)
    normal_hat = centred * inv_std
    normed = normal_hat * gain
    mixed_send[...] = (normed * gating).astype(BF16)
    mixed_copy = remote(mixed_send, other_mixed, 3, partner, me_ctx)
    mixed_copy.start()
    gate_scale = normed * slope_u
    hat_scale = gating * gain

    buckets = iota((128, 128), 0)
    own_head = iota((H, 128), 0) == own
    lines = []
    for block in range(REACH):
        chosen = jnp.where(buckets == bm_ref[block : block + 1, :], 1.0, 0.0)
        table = lax.dot_general(
            rab_ref[...],
            chosen,
            (((1,), (0,)), ((), ())),
            precision=lax.Precision.HIGHEST,
            preferred_element_type=F32,
        )
        lines.append(jnp.sum(jnp.where(own_head, table, 0.0), axis=0, keepdims=True) * 0.5)
    blank = jnp.zeros((1, 128), F32)
    for far in range(REACH + 1):
        current = lines[far] if far < REACH else blank
        before = lines[far - 1] if far > 0 else blank
        both = jnp.broadcast_to(jnp.concatenate([current, before], axis=1), (128, 256))
        tile = pltpu.roll(both, 0, 1, stride=1, stride_axis=0)[:, :128]
        bias[(REACH + 1 - far) * 128 : (REACH + 2 - far) * 128, :] = tile
    bias[:128, :] = jnp.zeros((128, 128), F32)
    bias[(REACH + 2) * 128 :, :] = jnp.zeros((128, 128), F32)
    dqt_total[...] = jnp.zeros(dqt_total.shape, F32)
    dkv_total[...] = jnp.zeros(dkv_total.shape, F32)

    taken = ro_ref[...].astype(F32)
    square = iota((128, 128), 0) == iota((128, 128), 1)
    slot_col = jnp.sum(jnp.where(square, taken, 0.0), axis=1, keepdims=True)
    place = iota((ROWS, SLOTS), 1)
    from_core = jnp.where(place < 256, core, 1 - core)
    from_dp = 2 * ((place >> 4) & 15) + from_core
    hot = jnp.where((from_dp * 4 + (place & 3)).astype(F32) == slot_col, 1.0, 0.0)
    column = iota((D, 256), 1)
    source_row = iota((D, 256), 0)
    spread_col = (column >> 4) * 32 + (column & 15)
    pick_own = jnp.where(source_row == spread_col + 16 * core, 1.0, 0.0).astype(BF16)
    pick_else = jnp.where(source_row == spread_col + 16 * (1 - core), 1.0, 0.0).astype(BF16)
    zero_core = jnp.broadcast_to(core, (ROWS, 128)) == 0

    def by_core(first, second):
        even = jnp.where(low, first, swap(second))
        odd = jnp.where(low, swap(first), second)
        return (
            jnp.where(zero_core, even, odd).astype(BF16),
            jnp.where(zero_core, odd, even).astype(BF16),
        )

    x_turned[:, :ROWS] = x.astype(F32).T.astype(BF16)
    x_copy.wait_recv()
    x_turned[:, ROWS:] = other_x[...].astype(F32).T.astype(BF16)
    mixed_copy.wait_recv()
    mixed_turned[:, :ROWS] = mixed_send[...].astype(F32).T.astype(BF16)
    mixed_turned[:, ROWS:] = other_mixed[...].astype(F32).T.astype(BF16)
    row_wait = many(sorted_rows, arrived, 0, N_Z - 1, partner, me_ctx)
    row_wait.wait_recv()
    for z in range(N_Z):
        cross_send[z] = arrived[z, 1 - core]
        gathered[z] = arrived[z, core]
    cross_copy = remote(cross_send, cross_got, 19, partner, me_ctx)
    cross_copy.start()
    cross_copy.wait_recv()
    gathered[N_Z:] = cross_got[...]
    owned = pick_pieces(hot, gathered[...].reshape(SLOTS, 128)).astype(BF16)
    grad_z = mm(owned, wo_ref[...], ((1,), (1,)))
    grad_hat = grad_z * hat_scale
    grad_attn = (
        grad_hat
        - jnp.mean(grad_hat, axis=1, keepdims=True)
        - normal_hat * jnp.mean(grad_hat * normal_hat, axis=1, keepdims=True)
    ) * inv_std
    stacked(grad_attn, g_send)
    g_got[own] = g_send[own]

    def g_copy(step):
        head = lax.rem(own + step, HALF)
        return remote(g_send.at[head], g_got.at[own], 4, me_dp, member(head, half))

    spread(HALF, g_copy)

    gate = grad_z * gate_scale
    gate_own = []
    for block in range(2):
        first = gate[:, 256 * block : 256 * block + 128]
        second = gate[:, 256 * block + 128 : 256 * block + 256]
        kept, given = by_core(first, second)
        gate_own.append(kept)
        early_send[:, 128 * block : 128 * block + 128] = given
    early_send[:, 256:] = mm(owned, pick_else).astype(BF16)
    early_copy = remote(early_send, other_early, 5, partner, me_ctx)
    early_copy.start()
    gate_own = jnp.concatenate(gate_own, axis=1)
    owned_own = mm(owned, pick_own).astype(BF16)
    gate = gate.astype(BF16)

    kv_wait = many(kv_got, kv_got, 2, N_CTX - 1, me_dp, next_ctx)
    kv_wait.wait_recv()
    for tile in range(TILES):
        flipped = kv_got[tile].astype(F32).T
        turned[:, tile * 128 : tile * 128 + 128] = flipped[:64].astype(BF16)
    early_copy.wait_recv()
    gate_both = jnp.concatenate([gate_own, other_early[:, :256]], axis=0)
    owned_both = jnp.concatenate([owned_own, other_early[:, 256:]], axis=0)
    first = mm(x_turned[...], gate_both)
    second = mm(mixed_turned[...], owned_both)
    left = iota((D, 128), 1) < 64
    for pair in range(2):
        gate_two = first[:, 128 * pair : 128 * pair + 128]
        out_two = second[:, 128 * pair : 128 * pair + 128]
        early_terms[2 * pair] = jnp.where(left, gate_two, swap(out_two)).astype(BF16)
        early_terms[2 * pair + 1] = jnp.where(left, swap(gate_two), out_two).astype(BF16)
    early_got[me_w] = early_terms[me_w]
    for step in (2, 1, 3):
        peer = lax.rem(me_w + step, 4)
        remote(
            early_terms.at[peer],
            early_got.at[me_w],
            6,
            2 * (me_z - me_w + peer) + core,
            me_ctx,
        ).start()

    q_wait = many(q_send, q_got, 9, HALF - 1, me_dp, next_ctx)
    g_wait = many(g_send, g_got, 4, HALF - 1, me_dp, next_ctx)
    q_wait.wait_recv()
    for index in range(HALF):
        block = q_got[index].astype(F32)
        pairs[index, :64] = jnp.where(top, block, 0.0).astype(BF16)
        pairs[index, 64:128] = jnp.where(top, swap(block), 0.0).astype(BF16)
    g_wait.wait_recv()
    for index in range(HALF):
        block = g_got[index].astype(F32)
        pairs[index, 128:192] = jnp.where(top, 0.0, swap(block)).astype(BF16)
        pairs[index, 192:] = jnp.where(top, 0.0, block).astype(BF16)
    edge_one = len_ref[0, 0]
    edge_two = edge_one + len_ref[0, 1]
    edge_three = edge_two + len_ref[0, 2]

    def meet(pair_index, index):
        keys = kv_got[pl.ds(2 * pair_index, 2)].reshape(256, 128)
        tile = member(index, half)
        place = tile * 128 + iota((1, 128), 1)
        first = jnp.where(place >= edge_one, edge_one, 0)
        first = jnp.where(place >= edge_two, edge_two, first)
        first = jnp.where(place >= edge_three, edge_three, first)
        both = mm(keys, pairs[index], ((1,), (1,)))
        row = pl.multiple_of((REACH + 1 - tile + 2 * pair_index) * 128, 128)
        scores = both[:, :128] + bias[pl.ds(row, 256), :]
        bent = jnp.tanh(scores)
        key_place = pair_index * 256 + iota((256, 128), 0)
        allowed = (key_place >= first) & (key_place <= place)
        rise = jnp.where(allowed, 1.0 + bent, 0.0)
        weights = scores * rise
        slopes = (both[:, 128:] * (rise + weights * (1.0 - bent))).astype(BF16)
        return jnp.concatenate([slopes, weights.astype(BF16)], axis=1)

    def ship(pair_index):
        done = dkv_total[pair_index] * (1.0 / 1024.0)
        dkv_send[pl.ds(2 * pair_index, 2)] = done.astype(BF16).reshape(2, 128, 128)
        for side in range(2):
            peer = 2 * pair_index + side

            @pl.when(peer != me_ctx)
            def _():
                remote(dkv_send.at[peer], dkv_got.at[me_ctx], 14, me_dp, peer).start()

    def one_round(step, carry):
        turn = lax.rem(own + 1 + step, 6)
        spots = [
            (turn, turn),
            (turn, turn + 1),
            (turn, turn + 2),
            (jnp.where(turn < 5, turn, 6), jnp.where(turn < 5, turn + 3, 6)),
            (jnp.where(turn < 4, turn, 11 - turn), jnp.where(turn < 4, turn + 4, 7)),
        ]
        found = [meet(pair_index, index) for pair_index, index in spots]
        for (pair_index, index), block in zip(spots, found):
            keys_turned = turned[:, pl.ds(pl.multiple_of(pair_index * 256, 256), 256)]
            dqt_total[index] += mm(keys_turned, block[:, :128])
        dkv_total[turn] += mm(
            jnp.concatenate(found[:3], axis=1), pairs[pl.ds(turn, 3)].reshape(768, 128)
        )
        for (pair_index, index), block in zip(spots[3:], found[3:]):
            dkv_total[pair_index] += mm(block, pairs[index])
        ship(turn)

        @pl.when(turn >= 4)
        def _():
            ship(11 - turn)

        return carry

    lax.fori_loop(0, 6, one_round, 0)
    dkv_got[me_ctx] = dkv_send[me_ctx]
    dqt_send[...] = (dqt_total[...] * (1.0 / 16384.0)).astype(BF16)
    dqt_got[own] = dqt_send[own]

    def dqt_copy(step):
        index = lax.rem(own + step, HALF)
        return remote(dqt_send.at[index], dqt_got.at[own], 15, me_dp, member(index, half))

    spread(HALF, dqt_copy)

    slot = slot_of(iota((SLOTS, ROWS), 0))
    back_hot = jnp.where(slot == ro_ref[...], 1.0, 0.0).astype(BF16)
    sent = jnp.where(iota((ROWS, 128), 0) == so_ref[...], 1.0, 0.0).astype(BF16)
    place = iota((ROWS, SLOTS), 1)
    spot = jnp.where(iota((ROWS, SLOTS), 0) == slot_of(place), 1.0, 0.0).astype(BF16)
    final_hot = mm(sent, spot)

    dkv_wait = many(dkv_send, dkv_got, 14, N_CTX - 1, me_dp, next_ctx)
    dqt_wait = many(dqt_send, dqt_got, 15, HALF - 1, me_dp, next_ctx)
    dkv_wait.wait_recv()
    grad_k = []
    grad_v = []
    for pair in range(H // 2):
        even = dkv_got[4 * pair].astype(F32) + dkv_got[4 * pair + 1].astype(F32)
        odd = dkv_got[4 * pair + 2].astype(F32) + dkv_got[4 * pair + 3].astype(F32)
        grad_k.append(jnp.where(low, even, swap(odd)))
        grad_v.append(jnp.where(low, swap(even), odd))
    after_v = jnp.concatenate(grad_v, axis=1) * slope_ref[:, :D]
    after_k = jnp.concatenate(grad_k, axis=1) * slope_ref[:, 2 * D :]
    late_own = []

    def split_late(wide, start):
        for block in range(2):
            kept, given = by_core(
                wide[:, 256 * block : 256 * block + 128],
                wide[:, 256 * block + 128 : 256 * block + 256],
            )
            late_own.append(kept)
            late_send[:, start + 128 * block : start + 128 * block + 128] = given

    split_late(after_v, 0)
    split_late(after_k, 256)
    late_copy = remote(
        late_send.at[:, pl.ds(0, 512)], other_late.at[:, pl.ds(0, 512)], 16, partner, me_ctx
    )
    late_copy.start()
    dqt_wait.wait_recv()
    after_q = dqt_got[...].reshape(D, 128).astype(F32).T * slope_ref[:, D : 2 * D]
    split_late(after_q, 512)
    query_copy = remote(
        late_send.at[:, pl.ds(512, 256)], other_late.at[:, pl.ds(512, 256)], 8, partner, me_ctx
    )
    query_copy.start()
    late_copy.wait_recv()
    late_both = jnp.concatenate(
        [jnp.concatenate(late_own[:4], axis=1), other_late[:, :512]], axis=0
    )
    late = mm(x_turned[...], late_both).astype(BF16)
    late_x[...] = late[:, :384].reshape(4, 128, 384)
    late_gx[me_x] = late_x[me_x]
    for step in (2, 1, 3):
        x, y = peers(step)
        remote(late_x.at[x], late_gx.at[me_x], 10, me_dp, 4 * x + me_y).start()
    query_copy.wait_recv()
    query_both = jnp.concatenate(
        [jnp.concatenate(late_own[4:], axis=1), other_late[:, 512:]], axis=0
    )
    late_q = mm(x_turned[...], query_both).astype(BF16)
    for x in range(4):
        for y in range(4):
            row = (4 * x + y) * 32
            late_y[y, 32 * x : 32 * x + 32, :128] = late[row : row + 32, 384:]
            late_y[y, 32 * x : 32 * x + 32, 128:] = late_q[row : row + 32, :]
    late_gy[me_y] = late_y[me_y]
    for step in (2, 1, 3):
        x, y = peers(step)
        remote(late_y.at[y], late_gy.at[me_y], 11, me_dp, 4 * me_x + y).start()
    after = jnp.concatenate([after_v, after_q, after_k], axis=1)
    grad_pre = jnp.concatenate([gate, after.astype(BF16)], axis=1)
    branch = mm(grad_pre, w_ref[...], ((1,), (1,))).astype(BF16)
    back_rows[...] = by_piece(mm(back_hot, branch)).astype(BF16).reshape(N_DP, 16, 128)
    returned[me_dp] = back_rows[me_dp]

    def back_copy(step):
        peer = far_dp(me_dp, step)
        return remote(back_rows.at[peer], returned.at[me_dp], 17, peer, me_ctx)

    spread(N_DP, back_copy)

    early_wait = many(early_terms, early_got, 6, 3, partner, me_ctx)
    early_wait.wait_recv()
    early_spread[...] = four(early_got).astype(BF16).reshape(N_CTX, 32, 128)
    early_parts[me_ctx] = early_spread[me_ctx]

    def early_part_copy(step):
        peer = lax.rem(me_ctx + step, N_CTX)
        return remote(early_spread.at[peer], early_parts.at[me_ctx], 7, me_dp, peer)

    spread(N_CTX, early_part_copy)

    late_wait = [
        many(late_x, late_gx, 10, 3, me_dp, next_ctx),
        many(late_y, late_gy, 11, 3, me_dp, next_ctx),
    ]
    for copy in late_wait:
        copy.wait_recv()
    fold(late_gx, late_mx)
    fold(late_gy, late_my)
    stage_two(late_mx, late_my, late_ex, late_ey, 12)
    back_wait = many(back_rows, returned, 17, N_DP - 1, next_dp, me_ctx)
    back_wait.wait_recv()
    arrival = pick_pieces(final_hot, returned[...].reshape(SLOTS, 128))
    rows_out[...] = (og_ref[...].astype(F32) + arrival).astype(BF16)
    rows_copy = pltpu.make_async_copy(rows_out, rows_hbm, load_sem.at[0])
    rows_copy.start()

    early_end = many(early_spread, early_parts, 7, N_CTX - 1, me_dp, next_ctx)
    early_end.wait_recv()
    early_sum = early_parts[0].astype(F32)
    for source in range(1, N_CTX):
        early_sum = early_sum + early_parts[source].astype(F32)
    late_end = [
        many(late_mx, late_ex, 12, 3, me_dp, next_ctx),
        many(late_my, late_ey, 13, 3, me_dp, next_ctx),
    ]
    for copy in late_end:
        copy.wait_recv()
    late_sum = jnp.concatenate([four(late_ex), four(late_ey)], axis=1)

    low = iota((32, 128), 1) < 64
    group = jnp.broadcast_to(me_w, (32, 128))
    for index in range(N_Z):
        if index < 4:
            block = jnp.where(group == index, early_sum, 0.0)
        else:
            spot = index - 4 if index < 8 else (index if index < 12 else index - 8)
            block = late_sum[:, (spot // 2) * 128 : (spot // 2) * 128 + 128]
            if spot % 2 == 1:
                block = swap(block)
        extra = early_sum
        if index % 4:
            extra = pltpu.roll(extra, 128 - 16 * (index % 4), 1)
        extra = jnp.where(group == index // 4, extra, 0.0)
        last_send[index] = jnp.where(low, block, extra).astype(BF16)
    last_got[me_z] = last_send[me_z]

    def last_copy(step):
        peer = lax.rem(me_z + far_first(step - 1), N_Z)
        return remote(last_send.at[peer], last_got.at[me_z], 18, 2 * peer + core, me_ctx)

    spread(N_Z, last_copy)
    last_wait = many(last_send, last_got, 18, N_Z - 1, 2 * lax.rem(me_z + 1, N_Z) + core, me_ctx)
    last_wait.wait_recv()
    total = last_got[0].astype(F32)
    for source in range(1, N_Z):
        total = total + last_got[source].astype(F32)
    total = total * (1.0 / 256.0)
    uvqk_out[...] = total[:, :64].astype(BF16)
    output_out[...] = total.T[64:80].astype(BF16)
    uvqk_copy = pltpu.make_async_copy(uvqk_out, uvqk_hbm, load_sem.at[1])
    output_copy = pltpu.make_async_copy(output_out, output_hbm, load_sem.at[2])
    uvqk_copy.start()
    output_copy.start()
    for copy in (
        row_wait,
        cross_copy,
        x_copy,
        kv_wait,
        mixed_copy,
        q_wait,
        g_wait,
        early_copy,
        dkv_wait,
        dqt_wait,
        late_copy,
        query_copy,
        early_wait,
        early_end,
        back_wait,
        last_wait,
        *late_wait,
        *late_end,
    ):
        copy.wait_send()
    rows_copy.wait()
    uvqk_copy.wait()
    output_copy.wait()


def finish_kernel(rows, uvqk, output, rows_out, uvqk_out, output_out, *scratch):
    held, sems = scratch[:3], scratch[3]
    taken = [
        pltpu.make_async_copy(source, target, sems.at[number])
        for number, (source, target) in enumerate(zip((rows, uvqk, output), held))
    ]
    given = [
        pltpu.make_async_copy(source, target, sems.at[3 + number])
        for number, (source, target) in enumerate(zip(held, (rows_out, uvqk_out, output_out)))
    ]
    for copy in taken:
        copy.start()
    for first, second in zip(taken, given):
        first.wait()
        second.start()
    for copy in given:
        copy.wait()


def bf16(*shape):
    return jax.ShapeDtypeStruct(shape, BF16)


def local(
    inputs,
    attn_out,
    out_grad,
    w_uvqk,
    w_output,
    norm_gain,
    rab_table,
    bucket_map,
    lengths,
    send_order,
    recv_order,
):
    taken = (
        inputs,
        attn_out,
        out_grad,
        w_uvqk,
        w_output,
        norm_gain.reshape(1, D),
        rab_table,
        bucket_map.reshape(8, 128),
        send_order,
        recv_order,
    )
    anywhere = pl.BlockSpec(memory_space=pl.ANY)
    scratch = [pltpu.VMEM(array.shape, array.dtype) for array in taken]
    for shape, kind in (
        ((N_Z, 2, 16, 128), BF16),
        ((N_Z, 2, 16, 128), BF16),
        ((N_Z, 16, 128), BF16),
        ((N_Z, 16, 128), BF16),
        ((N_DP, 16, 128), BF16),
        ((H, 128, 128), BF16),
        ((N_CTX, 128, 128), BF16),
        *(((HALF, 64, 128), BF16),) * 4,
        (((REACH + 3) * 128, 128), F32),
        ((64, TILES * 128), BF16),
        ((HALF, 256, 128), BF16),
        ((HALF, 64, 128), F32),
        ((PAIRS, 256, 128), F32),
        ((N_CTX, 128, 128), BF16),
        ((N_CTX, 128, 128), BF16),
        ((HALF, 64, 128), BF16),
        ((HALF, 64, 128), BF16),
        ((ROWS, 3 * D), F32),
        ((N_DP, 16, 128), BF16),
        ((N_DP, 16, 128), BF16),
        ((ROWS, D), BF16),
        ((ROWS, EARLY), BF16),
        ((ROWS, LATE), BF16),
        ((ROWS, D), BF16),
        ((ROWS, D), BF16),
        ((ROWS, EARLY), BF16),
        ((ROWS, LATE), BF16),
        ((D, 2 * ROWS), BF16),
        ((D, 2 * ROWS), BF16),
        ((4, D, 128), BF16),
        ((4, D, 128), BF16),
        ((N_CTX, 32, 128), BF16),
        ((N_CTX, 32, 128), BF16),
        *(((4, 128, LATE // 2), BF16),) * 4,
        *(((4, 32, LATE // 2), BF16),) * 4,
        ((N_Z, 32, 128), BF16),
        ((N_Z, 32, 128), BF16),
        ((ROWS, D), BF16),
        ((32, 64), BF16),
        ((16, 32), BF16),
    ):
        scratch.append(pltpu.VMEM(shape, kind))
    scratch += [
        pltpu.SemaphoreType.DMA((10,)),
        pltpu.SemaphoreType.DMA((20,)),
        pltpu.SemaphoreType.DMA((20,)),
    ]
    shapes = (bf16(ROWS, D), bf16(32, 64), bf16(16, 32))
    results = pl.pallas_call(
        layer_kernel,
        out_shape=shapes,
        in_specs=[pl.BlockSpec(memory_space=pltpu.SMEM)]
        + [anywhere] * len(taken),
        out_specs=(anywhere,) * 3,
        scratch_shapes=scratch,
        compiler_params=pltpu.CompilerParams(
            collective_id=0, has_side_effects=True, vmem_limit_bytes=LIMIT
        ),
    )(lengths, *taken)
    rows, uvqk, output = pl.pallas_call(
        finish_kernel,
        out_shape=shapes,
        in_specs=[anywhere] * 3,
        out_specs=(anywhere,) * 3,
        scratch_shapes=[pltpu.VMEM(shape.shape, shape.dtype) for shape in shapes]
        + [pltpu.SemaphoreType.DMA((6,))],
        compiler_params=pltpu.CompilerParams(vmem_limit_bytes=LIMIT),
    )(*results)
    return rows, uvqk, output.T


def solution(mesh):
    in_specs = (
        P(("dp", "ctx"), None),
        P(("dp", "ctx"), None),
        P(("dp", "ctx"), None),
        P(),
        P(),
        P(),
        P(),
        P(),
        P("dp", None),
        P(("dp", "ctx"), None),
        P(("dp", "ctx"), None),
    )
    out_specs = (P(("dp", "ctx"), None), P("ctx", "dp"), P("ctx", "dp"))
    return jax.shard_map(local, mesh=mesh, in_specs=in_specs, out_specs=out_specs, check_vma=False)
```
